256 devices in a mesh: leaf: 32 (over z, y), head: 8 (over x, core).
Axes of the slice: x: 4, y: 4, z: 8, core: 2. Of those that a mesh axis runs over, the one named last changes fastest.
Arguments:
- normed_input: bfloat16 [12288, 1024], P('leaf'), may hold values from -6 to 6
- queries: bfloat16 [12288, 2048], P('leaf', 'head'), may hold values from -128 to 128
- keys: bfloat16 [12288, 1024], P('leaf', 'head'), may hold values from -4 to 4
- values: bfloat16 [12288, 1024], P('leaf', 'head'), may hold values from -6 to 6
- grad_out: bfloat16 [12288, 1024], P('leaf'), may hold values from -6 to 6
- query_weight: bfloat16 [1024, 2048], P(None, 'head'), may hold values from -0.1875 to 0.1875
- key_projection_matrix: bfloat16 [1024, 1024], P(None, 'head'), may hold values from -0.1875 to 0.1875
- value_projection_matrix: bfloat16 [1024, 1024], P(None, 'head'), may hold values from -0.1875 to 0.1875
- output_weight: bfloat16 [2048, 1024], P('head'), may hold values from -0.125 to 0.125
- ancestors: int32 [96, 16], replicated, may hold values from -1 to 95, as said below
Outputs:
- input_grad: bfloat16 [12288, 1024], P('leaf', 'head')
- query_weight_grad: float32 [1024, 2048], P('leaf', 'head')
- key_weight_grad: float32 [1024, 1024], P('leaf', 'head')
- value_weight_grad: float32 [1024, 1024], P('leaf', 'head')
- output_weight_grad: float32 [2048, 1024], P('head', 'leaf')
The draws below stay inside these ranges and needn't reach their ends.
Inputs may be any that keep to these rules, and one draw needn't show every extreme that they name: `ancestors`: row b lists b itself, then its parent, its parent's parent and so on to the root, then -1 in the remaining slots; every parent is an earlier block; some row lists exactly 16 blocks.
All inputs are finite; a program needn't handle non-finite values.
Results may differ from the reference program's by a relative error of at most 0.034.
Values may be sent and summed in bfloat16 or wider, within the bound.
No kernel may reach another device: no remote copies, remote signals or barrier semaphores. Data moves between devices by JAX's collectives and lax.ppermute only.
A program may use at most 128 MiB of HBM per device.

```python
import jax
import jax.numpy as jnp
from jax import lax

MODEL_WIDTH = 1024
QUERY_HEADS = 16
KEY_VALUE_HEADS = 8
HEAD_WIDTH = 128
NODE_BLOCK_TOKENS = 128
PATH_BLOCK_LIMIT = 16
TREE_BLOCKS = 96
TREE_TOKENS = 12288


def shared_keys(key):
    block_offset = jnp.clip(jax.random.normal(key, (TREE_TOKENS, KEY_VALUE_HEADS * HEAD_WIDTH), jnp.float32), -4.0, 4.0)
    return block_offset


def draw_keys(key, part):
    block_offset = shared_keys(key)
    final_output = block_offset
    return final_output.astype(jnp.bfloat16)


def draw_queries(key, part):
    key = jax.random.fold_in(key, 22)
    fresh = jnp.clip(jax.random.normal(key, (TREE_TOKENS, QUERY_HEADS * HEAD_WIDTH), jnp.float32), -4.0, 4.0)
    final_output = fresh
    return final_output.astype(jnp.bfloat16)


def draw_ancestors(key, part):
    key = jax.random.fold_in(key, 31)
    keep_key, pick_key, fall_key = jax.random.split(key, 3)
    keep = jax.random.randint(keep_key, (TREE_BLOCKS,), 0, 4)
    pick = jax.random.randint(pick_key, (TREE_BLOCKS,), 0, 1 << 30)
    fall = jax.random.randint(fall_key, (TREE_BLOCKS,), 0, PATH_BLOCK_LIMIT - 1)

    def visit(depth, block_id):
        branch = pick[block_id] % jnp.maximum(block_id, 1)
        parent = jnp.where(keep[block_id] < 3, block_id - 1, branch)
        parent = jnp.where(depth[jnp.maximum(parent, 0)] >= PATH_BLOCK_LIMIT - 1, fall[block_id], parent)
        parent = jnp.where(block_id < PATH_BLOCK_LIMIT, block_id - 1, parent)
        level = jnp.where(block_id == 0, 0, depth[jnp.maximum(parent, 0)] + 1)
        depth = depth.at[block_id].set(level.astype(jnp.int32))
        return (depth, parent.astype(jnp.int32))
    depth, parents = lax.scan(visit, jnp.zeros((TREE_BLOCKS,), jnp.int32), jnp.arange(TREE_BLOCKS, dtype=jnp.int32))
    current = jnp.arange(TREE_BLOCKS, dtype=jnp.int32)
    columns = []
    for position in range(PATH_BLOCK_LIMIT):
        columns.append(current)
        current = jnp.where(current >= 0, parents[jnp.maximum(current, 0)], -1).astype(jnp.int32)
    return jnp.stack(columns, axis=1).astype(jnp.int32)


def spiked(array, stream_key, source, target, parts, factor):
    def block_of(dim):
        return (jnp.arange(array.shape[dim]) // (array.shape[dim] // parts)).reshape((-1,) + (1,) * (array.ndim - 1 - dim))

    one_side = jax.random.permutation(stream_key, parts)[block_of(target)]
    other_side = (block_of(target) + parts // 2) % parts
    return jnp.where((block_of(source) == one_side) | (block_of(source) == other_side), factor * array, array)


def level_of(rng, dims, pieces, smallest, top_value):
    level, own = 1.0, jax.random.fold_in(rng, 6)
    for dim, blocks in pieces:
        draws = jnp.exp(jax.random.uniform(jax.random.fold_in(own, dim), (blocks,), jnp.float32, smallest / len(pieces), top_value / len(pieces)))
        level = level * jnp.repeat(draws, dims[dim] // blocks).reshape([-1 if axis == dim else 1 for axis in range(len(dims))])
    return level


def normal_values(key, dims, width, reach, pieces=(), kind=jnp.bfloat16):
    gain = level_of(key, dims, pieces, -0.22, 0.18) if pieces else 1.0
    values = jax.random.normal(key, dims, jnp.float32) * width * gain
    return jnp.minimum(jnp.maximum(values, -reach), reach).astype(kind)


def gaussian_with(rng, shape, deviation, limit, pieces, heavy, kind=jnp.bfloat16):
    result = deviation * jax.random.normal(rng, shape, jnp.float32)
    if pieces:
        result = result * level_of(rng, shape, pieces, -0.22, 0.18)
    return jnp.clip(spiked(result, jax.random.fold_in(rng, 3), *heavy), -limit, limit).astype(kind)


def setup_inputs(seed: int = 0) -> dict:
    key_of = jax.random.split(jax.random.key(seed), 11)
    return {
        "normed_input": gaussian_with(key_of[0], (TREE_TOKENS, MODEL_WIDTH), 1.0, 6.0, ((0, 32),), (0, 1, 32, 2.75)),
        "queries": draw_queries(jax.random.fold_in(key_of[10], 71), 0),
        "keys": draw_keys(jax.random.fold_in(key_of[10], 71), 0),
        "values": normal_values(key_of[3], (TREE_TOKENS, KEY_VALUE_HEADS * HEAD_WIDTH), 1.0, 6.0, ((0, 32), (1, 8))),
        "grad_out": gaussian_with(key_of[4], (TREE_TOKENS, MODEL_WIDTH), 1.0, 6.0, ((0, 32),), (0, 1, 32, 2.75)),
        "query_weight": normal_values(key_of[5], (MODEL_WIDTH, QUERY_HEADS * HEAD_WIDTH), MODEL_WIDTH ** -0.5, 0.1875, ((1, 8),)),
        "key_projection_matrix": normal_values(key_of[6], (MODEL_WIDTH, KEY_VALUE_HEADS * HEAD_WIDTH), MODEL_WIDTH ** -0.5, 0.1875, ((1, 8),)),
        "value_projection_matrix": normal_values(key_of[7], (MODEL_WIDTH, KEY_VALUE_HEADS * HEAD_WIDTH), MODEL_WIDTH ** -0.5, 0.1875, ((1, 8),)),
        "output_weight": normal_values(key_of[8], (QUERY_HEADS * HEAD_WIDTH, MODEL_WIDTH), (QUERY_HEADS * HEAD_WIDTH) ** -0.5, 0.125, ((0, 8),)),
        "ancestors": draw_ancestors(jax.random.fold_in(key_of[10], 71), 0),
    }


def tile_visibility(anc_row, block_id, block_len):
    valid = anc_row >= 0
    itself = anc_row == block_id
    places = jnp.arange(block_len)
    causal = places[:, None] >= places[None, :]
    allowed = valid[None, :, None] & (jnp.logical_not(itself)[None, :, None] | causal[:, None, :])
    return allowed.reshape(block_len, -1)


def attend_block(query_tile, grad_tile, key_block_slice, value_block_slice, visible, score_scale):
    f32 = jnp.float32
    scores = jnp.einsum('bhgd,lhd->hgbl', query_tile.astype(f32), key_block_slice.astype(f32)) * score_scale
    scores = jnp.where(visible[None, None], scores, -jnp.inf)
    row_max = jnp.max(scores, axis=-1, keepdims=True)
    row_total = jnp.sum(jnp.exp(scores - row_max), axis=-1, keepdims=True)
    log_total = row_max + jnp.log(row_total)
    weights = jnp.exp(scores - log_total)
    probabilities = weights.astype(jnp.bfloat16)
    attended = jnp.einsum('hgbl,lhd->bhgd', probabilities.astype(f32), value_block_slice.astype(f32)).astype(jnp.bfloat16)
    row_delta = jnp.einsum('bhgd,bhgd->hgb', grad_tile.astype(f32), attended.astype(f32))
    grad_probs = jnp.einsum('bhgd,lhd->hgbl', grad_tile.astype(f32), value_block_slice.astype(f32))
    dscore = (weights * (grad_probs - row_delta[..., None]) * score_scale).astype(jnp.bfloat16)
    grad_query = jnp.einsum('hgbl,lhd->bhgd', dscore.astype(f32), key_block_slice.astype(f32)).astype(jnp.bfloat16)
    key_contribution = jnp.einsum('hgbl,bhgd->lhd', dscore.astype(f32), query_tile.astype(f32))
    value_contribution = jnp.einsum('hgbl,bhgd->lhd', probabilities.astype(f32), grad_tile.astype(f32))
    return attended, grad_query, key_contribution, value_contribution


def reference(normed_input, queries, keys, values, grad_out, query_weight, key_projection_matrix, value_projection_matrix, output_weight, ancestors):
    query_group_count = QUERY_HEADS // KEY_VALUE_HEADS
    score_scale = HEAD_WIDTH ** -0.5
    attention_grad = jnp.dot(grad_out, output_weight.T, preferred_element_type=jnp.float32).astype(jnp.bfloat16)
    blocked_queries = queries.reshape(TREE_BLOCKS, NODE_BLOCK_TOKENS, KEY_VALUE_HEADS, query_group_count, HEAD_WIDTH)
    gradient_blocks = attention_grad.reshape(TREE_BLOCKS, NODE_BLOCK_TOKENS, KEY_VALUE_HEADS, query_group_count, HEAD_WIDTH)
    blocked_keys = keys.reshape(TREE_BLOCKS, NODE_BLOCK_TOKENS, KEY_VALUE_HEADS, HEAD_WIDTH)
    blocked_values = values.reshape(TREE_BLOCKS, NODE_BLOCK_TOKENS, KEY_VALUE_HEADS, HEAD_WIDTH)

    def visit(carry, block_id):
        key_running_sum, value_running_sum = carry
        anc_row = ancestors[block_id]
        guarded_rows = jnp.maximum(anc_row, 0).astype(jnp.int32)
        key_block_slice = blocked_keys[guarded_rows].reshape(PATH_BLOCK_LIMIT * NODE_BLOCK_TOKENS, KEY_VALUE_HEADS, HEAD_WIDTH)
        value_block_slice = blocked_values[guarded_rows].reshape(PATH_BLOCK_LIMIT * NODE_BLOCK_TOKENS, KEY_VALUE_HEADS, HEAD_WIDTH)
        visible = tile_visibility(anc_row, block_id, NODE_BLOCK_TOKENS)
        attended, grad_query, key_contribution, value_contribution = attend_block(
            blocked_queries[block_id], gradient_blocks[block_id], key_block_slice, value_block_slice, visible, score_scale)
        key_running_sum = key_running_sum.at[guarded_rows].add(key_contribution.reshape(PATH_BLOCK_LIMIT, NODE_BLOCK_TOKENS, KEY_VALUE_HEADS, HEAD_WIDTH))
        value_running_sum = value_running_sum.at[guarded_rows].add(value_contribution.reshape(PATH_BLOCK_LIMIT, NODE_BLOCK_TOKENS, KEY_VALUE_HEADS, HEAD_WIDTH))
        return (key_running_sum, value_running_sum), (attended, grad_query)

    zero_filled = jnp.zeros((TREE_BLOCKS, NODE_BLOCK_TOKENS, KEY_VALUE_HEADS, HEAD_WIDTH), jnp.float32)
    (key_running_sum, value_running_sum), (attended, grad_query) = lax.scan(
        visit, (zero_filled, zero_filled), jnp.arange(TREE_BLOCKS, dtype=jnp.int32))
    attn_out = attended.reshape(TREE_TOKENS, QUERY_HEADS * HEAD_WIDTH)
    grad_q = grad_query.reshape(TREE_TOKENS, QUERY_HEADS * HEAD_WIDTH)
    key_gradient = key_running_sum.reshape(TREE_TOKENS, KEY_VALUE_HEADS * HEAD_WIDTH).astype(jnp.bfloat16)
    value_gradient = value_running_sum.reshape(TREE_TOKENS, KEY_VALUE_HEADS * HEAD_WIDTH).astype(jnp.bfloat16)
    output_weight_grad = jnp.dot(attn_out.T, grad_out, preferred_element_type=jnp.float32)
    query_weight_grad = jnp.dot(normed_input.T, grad_q, preferred_element_type=jnp.float32)
    key_weight_grad = jnp.dot(normed_input.T, key_gradient, preferred_element_type=jnp.float32)
    value_weight_grad = jnp.dot(normed_input.T, value_gradient, preferred_element_type=jnp.float32)
    input_sum = jnp.dot(grad_q, query_weight.T, preferred_element_type=jnp.float32)
    input_sum = input_sum + jnp.dot(key_gradient, key_projection_matrix.T, preferred_element_type=jnp.float32)
    input_sum = input_sum + jnp.dot(value_gradient, value_projection_matrix.T, preferred_element_type=jnp.float32)
    input_grad = input_sum.astype(jnp.bfloat16)
    return input_grad, query_weight_grad, key_weight_grad, value_weight_grad, output_weight_grad
```

```python
import functools

import jax
import jax.numpy as jnp
from jax import lax
from jax.experimental import pallas as pl
from jax.experimental.pallas import tpu as pltpu
from jax.sharding import Mesh, PartitionSpec as P

HEAD_WIDTH = 128
BLOCK = 128
GROUP = 2
NZ, NY = 8, 4
DEV_BLOCKS = 3
ROW_BLOCKS = NY * DEV_BLOCKS
COL_BLOCKS = NZ * DEV_BLOCKS
PATH = 16
PAIR = GROUP * BLOCK
SCALE = HEAD_WIDTH ** (-0.5)
NEG = -1e30
STAT_ROWS = 16
VMEM_LIMIT = 48 * 1024 * 1024

f32 = jnp.float32
bf16 = jnp.bfloat16


def dot_nt(a, b):
    return lax.dot_general(a, b, (((1,), (1,)), ((), ())), preferred_element_type=f32)


def dot_nn(a, b):
    return jnp.dot(a, b, preferred_element_type=f32)


def fold(x, op):
    return op(x.reshape(BLOCK // 8, 8, PAIR), axis=0)


def collect(anc_ref, list_ref, block, y):
    def step(j, count):
        c = anc_ref[block, j]
        hit = jnp.logical_and(c >= 0, lax.rem(lax.div(c, DEV_BLOCKS), NY) == y)
        list_ref[count] = lax.div(c, ROW_BLOCKS) * DEV_BLOCKS + lax.rem(c, DEV_BLOCKS)
        return count + hit.astype(jnp.int32)

    return lax.fori_loop(0, PATH, step, jnp.int32(0))


def stack_queries(qd_refs, q_scr, d_scr):
    for s in range(NY):
        for r in range(DEV_BLOCKS):
            for h in range(GROUP):
                rows = slice(r * BLOCK, (r + 1) * BLOCK)
                put = slice(h * BLOCK, (h + 1) * BLOCK)
                cols = slice(h * HEAD_WIDTH, (h + 1) * HEAD_WIDTH)
                dcols = slice(PAIR + h * HEAD_WIDTH, PAIR + (h + 1) * HEAD_WIDTH)
                q_scr[s * DEV_BLOCKS + r, put, :] = qd_refs[s][rows, cols]
                d_scr[s * DEV_BLOCKS + r, put, :] = qd_refs[s][rows, dcols]


def place_of(i, z, y):
    s = lax.div(i, DEV_BLOCKS)
    r = lax.rem(i, DEV_BLOCKS)
    at = lax.rem(y - s + NY, NY) * DEV_BLOCKS + r
    own = jnp.where(s == 0, z * DEV_BLOCKS + r, -1)
    return at, z * ROW_BLOCKS + at, own


def score_tile(k, q, is_own):
    s = dot_nt(k, q) * SCALE
    key_at = lax.broadcasted_iota(jnp.int32, (BLOCK, PAIR), 0)
    query_at = lax.rem(lax.broadcasted_iota(jnp.int32, (BLOCK, PAIR), 1), BLOCK)
    return jnp.where(jnp.logical_and(is_own, key_at > query_at), NEG, s)


def stats_kernel(pos_ref, anc_ref, kv_ref, qd0, qd1, qd2, qd3, out_ref, q_scr, d_scr, s_scr, list_ref):
    z, y = pos_ref[0], pos_ref[1]
    stack_queries((qd0, qd1, qd2, qd3), q_scr, d_scr)

    def one_block(i, _):
        at, block, own = place_of(i, z, y)
        count = collect(anc_ref, list_ref, block, y)
        q = q_scr[i]
        d = d_scr[i]

        def scores(j, top):
            slot = list_ref[j]
            rows = pl.ds(pl.multiple_of(slot * BLOCK, BLOCK), BLOCK)
            s = score_tile(kv_ref[rows, :HEAD_WIDTH], q, slot == own)
            s_scr[j] = s
            return jnp.maximum(top, fold(s, jnp.max))

        top = lax.fori_loop(0, count, scores, jnp.full((8, PAIR), NEG, f32))
        m = jnp.max(top, axis=0, keepdims=True)

        def sums(j, carry):
            total, dsum = carry
            slot = list_ref[j]
            rows = pl.ds(pl.multiple_of(slot * BLOCK, BLOCK), BLOCK)
            p = jnp.exp(s_scr[j] - m)
            g = dot_nt(kv_ref[rows, HEAD_WIDTH:], d)
            return total + fold(p, jnp.sum), dsum + fold(p * g, jnp.sum)

        zero = jnp.zeros((8, PAIR), f32)
        total, dsum = lax.fori_loop(0, count, sums, (zero, zero))
        out_ref[pl.ds(at, 1), :] = m
        out_ref[pl.ds(STAT_ROWS + at, 1), :] = jnp.sum(total, axis=0, keepdims=True)
        out_ref[pl.ds(2 * STAT_ROWS + at, 1), :] = jnp.sum(dsum, axis=0, keepdims=True)
        return 0

    lax.fori_loop(0, ROW_BLOCKS, one_block, 0)


def grads_kernel(
    pos_ref, anc_ref, kv_ref, qd0, qd1, qd2, qd3, st0, st1, st2, st3,
    row_ref, col_ref,
    q_scr, d_scr, kt_scr, vt_scr, o_scr, dq_scr, dk_scr, dv_scr, list_ref,
):
    z, y = pos_ref[0], pos_ref[1]
    stats = (st0, st1, st2, st3)
    stack_queries((qd0, qd1, qd2, qd3), q_scr, d_scr)

    def prepare(c, _):
        rows = pl.ds(pl.multiple_of(c * BLOCK, BLOCK), BLOCK)
        kt_scr[c] = kv_ref[rows, :HEAD_WIDTH].T
        vt_scr[c] = kv_ref[rows, HEAD_WIDTH:].T
        dk_scr[c] = jnp.zeros((BLOCK, HEAD_WIDTH), f32)
        dv_scr[c] = jnp.zeros((BLOCK, HEAD_WIDTH), f32)
        return 0

    lax.fori_loop(0, COL_BLOCKS, prepare, 0)

    def one_block(i, _):
        at, block, own = place_of(i, z, y)
        count = collect(anc_ref, list_ref, block, y)
        q = q_scr[i]
        d = d_scr[i]
        tops = [st[pl.ds(at, 1), :] for st in stats]
        m = functools.reduce(jnp.maximum, tops)
        factors = [jnp.exp(t - m) for t in tops]
        total = sum(st[pl.ds(STAT_ROWS + at, 1), :] * f for st, f in zip(stats, factors))
        dsum = sum(st[pl.ds(2 * STAT_ROWS + at, 1), :] * f for st, f in zip(stats, factors))
        lse = m + jnp.log(total)
        delta = dsum / total
        o_scr[...] = jnp.zeros((HEAD_WIDTH, PAIR), f32)
        dq_scr[...] = jnp.zeros((HEAD_WIDTH, PAIR), f32)

        def one_key(j, _):
            slot = list_ref[j]
            rows = pl.ds(pl.multiple_of(slot * BLOCK, BLOCK), BLOCK)
            s = score_tile(kv_ref[rows, :HEAD_WIDTH], q, slot == own)
            w = jnp.exp(s - lse)
            p = w.astype(bf16)
            g = dot_nt(kv_ref[rows, HEAD_WIDTH:], d)
            ds = (w * (g - delta) * SCALE).astype(bf16)
            o_scr[...] += dot_nn(vt_scr[slot], p)
            dq_scr[...] += dot_nn(kt_scr[slot], ds)
            dk_scr[slot] += dot_nn(ds, q)
            dv_scr[slot] += dot_nn(p, d)
            return 0

        lax.fori_loop(0, count, one_key, 0)
        t = lax.rem(NY - lax.div(i, DEV_BLOCKS), NY)
        cols = pl.ds(pl.multiple_of(lax.rem(i, DEV_BLOCKS) * BLOCK, BLOCK), BLOCK)
        for h in range(GROUP):
            heads = slice(h * BLOCK, (h + 1) * BLOCK)
            row_ref[t, h * HEAD_WIDTH : (h + 1) * HEAD_WIDTH, cols] = o_scr[:, heads].astype(bf16)
            row_ref[t, PAIR + h * HEAD_WIDTH : PAIR + (h + 1) * HEAD_WIDTH, cols] = dq_scr[
                :, heads
            ].astype(bf16)
        return 0

    lax.fori_loop(0, ROW_BLOCKS, one_block, 0)

    def finish(c, _):
        rows = pl.ds(pl.multiple_of(c * BLOCK, BLOCK), BLOCK)
        col_ref[rows, :HEAD_WIDTH] = dk_scr[c].astype(bf16)
        col_ref[rows, HEAD_WIDTH:] = dv_scr[c].astype(bf16)
        return 0

    lax.fori_loop(0, COL_BLOCKS, finish, 0)


SMEM_SPEC = pl.BlockSpec(memory_space=pltpu.SMEM)
VMEM_SPEC = pl.BlockSpec(memory_space=pltpu.VMEM)


def stats_call(pos, anc, kv, qds):
    return pl.pallas_call(
        stats_kernel,
        out_shape=jax.ShapeDtypeStruct((3 * STAT_ROWS, PAIR), f32),
        in_specs=[SMEM_SPEC] * 2 + [VMEM_SPEC] * 5,
        out_specs=VMEM_SPEC,
        scratch_shapes=[
            pltpu.VMEM((ROW_BLOCKS, PAIR, HEAD_WIDTH), bf16),
            pltpu.VMEM((ROW_BLOCKS, PAIR, HEAD_WIDTH), bf16),
            pltpu.VMEM((PATH, BLOCK, PAIR), f32),
            pltpu.SMEM((PATH + 1,), jnp.int32),
        ],
        compiler_params=pltpu.CompilerParams(vmem_limit_bytes=VMEM_LIMIT),
        name="stats",
    )(pos, anc, kv, *qds)


def grads_call(pos, anc, kv, qds, stats):
    return pl.pallas_call(
        grads_kernel,
        out_shape=(
            jax.ShapeDtypeStruct((NY, 2 * PAIR, DEV_BLOCKS * BLOCK), bf16),
            jax.ShapeDtypeStruct((COL_BLOCKS * BLOCK, 2 * HEAD_WIDTH), bf16),
        ),
        in_specs=[SMEM_SPEC] * 2 + [VMEM_SPEC] * 9,
        out_specs=(VMEM_SPEC, VMEM_SPEC),
        scratch_shapes=[
            pltpu.VMEM((ROW_BLOCKS, PAIR, HEAD_WIDTH), bf16),
            pltpu.VMEM((ROW_BLOCKS, PAIR, HEAD_WIDTH), bf16),
            pltpu.VMEM((COL_BLOCKS, HEAD_WIDTH, BLOCK), bf16),
            pltpu.VMEM((COL_BLOCKS, HEAD_WIDTH, BLOCK), bf16),
            pltpu.VMEM((HEAD_WIDTH, PAIR), f32),
            pltpu.VMEM((HEAD_WIDTH, PAIR), f32),
            pltpu.VMEM((COL_BLOCKS, BLOCK, HEAD_WIDTH), f32),
            pltpu.VMEM((COL_BLOCKS, BLOCK, HEAD_WIDTH), f32),
            pltpu.SMEM((PATH + 1,), jnp.int32),
        ],
        compiler_params=pltpu.CompilerParams(vmem_limit_bytes=VMEM_LIMIT),
        name="grads",
    )(pos, anc, kv, *qds, *stats)


def shift(x, axis, size, by):
    return lax.ppermute(x, axis, [(i, (i + by) % size) for i in range(size)])


def per_device(
    nx, nc, normed_input, queries, keys, values, grad_out, query_weight, key_weight, value_weight, output_weight, ancestors
):
    z, y = lax.axis_index("z"), lax.axis_index("y")
    x, c = lax.axis_index("x"), lax.axis_index("c")
    rows = queries.shape[0]
    model = grad_out.shape[1]
    pos = jnp.stack([z, y]).astype(jnp.int32)

    kv = lax.all_gather(jnp.concatenate([keys, values], axis=1), "z", axis=0, tiled=True)
    attn_grad = dot_nt(grad_out, output_weight).astype(bf16)
    mine = jnp.concatenate([queries, attn_grad], axis=1)
    qds = [mine] + [shift(mine, "y", NY, s) for s in range(1, NY)]

    heads = nx * nc
    width = model // heads

    def laid_out(w):
        w = w.reshape(nx, nc, width, w.shape[1])
        w = jnp.roll(jnp.roll(w, -x, axis=0), -c, axis=1)
        return w.transpose(1, 0, 2, 3).reshape(model, w.shape[3])

    wq = laid_out(query_weight)
    wkv = laid_out(jnp.concatenate([key_weight, value_weight], axis=1))

    own = stats_call(pos, ancestors, kv, qds)
    stats = [own] + [shift(own, "y", NY, s) for s in range(1, NY)]
    row_part, col_part = grads_call(pos, ancestors, kv, qds, stats)

    got = [shift(row_part[s], "y", NY, s) for s in range(1, NY)]
    col_got = lax.all_to_all(col_part.reshape(NZ, rows, 2 * HEAD_WIDTH), "z", 0, 0, tiled=True)
    row_sum = sum((g.astype(f32) for g in got), row_part[0].astype(f32)).astype(bf16)
    attn_t, dq_t = row_sum[:PAIR], row_sum[PAIR:]
    dkv = jnp.sum(col_got.astype(f32), axis=0).astype(bf16)

    part = lax.dot_general(dq_t, wq, (((0,), (1,)), ((), ())), preferred_element_type=f32)
    part = part + dot_nt(dkv, wkv)
    part = part.reshape(rows, nc, nx * width)
    keep = part[:, 0]
    for s in range(1, nc):
        keep = keep + shift(part[:, s].astype(bf16), "c", nc, s).astype(f32)
    input_grad = keep[:, :width]
    for s in range(1, nx):
        piece = keep[:, s * width : (s + 1) * width].astype(bf16)
        input_grad = input_grad + shift(piece, "x", nx, s).astype(f32)
    input_grad = input_grad.astype(bf16)

    contract_rows = (((0,), (0,)), ((), ()))
    q_part = lax.dot_general(normed_input, dq_t, (((0,), (1,)), ((), ())), preferred_element_type=f32)
    kv_part = lax.dot_general(normed_input, dkv, contract_rows, preferred_element_type=f32)
    o_part = lax.dot_general(grad_out, attn_t, (((0,), (1,)), ((), ())), preferred_element_type=f32)
    parts = jnp.concatenate([q_part.astype(bf16), o_part.astype(bf16), kv_part.astype(bf16)], axis=1)
    leaves = NZ * NY
    parts = parts.reshape(leaves, model // leaves, parts.shape[1])
    sums = jnp.sum(lax.all_to_all(parts, ("z", "y"), 0, 0, tiled=True).astype(f32), axis=0)
    return (
        input_grad,
        sums[:, :PAIR],
        sums[:, 2 * PAIR : 2 * PAIR + HEAD_WIDTH],
        sums[:, 2 * PAIR + HEAD_WIDTH :],
        sums[:, PAIR : 2 * PAIR].T,
    )


def solution(mesh):
    heads = mesh.shape["head"]
    nc = 2 if heads % 2 == 0 else 1
    nx = heads // nc
    grid = Mesh(mesh.devices.reshape(NZ, NY, nx, nc), ("z", "y", "x", "c"))
    leaf, head = ("z", "y"), ("x", "c")
    return jax.shard_map(
        functools.partial(per_device, nx, nc),
        mesh=grid,
        in_specs=(
            P(leaf, None),
            P(leaf, head),
            P(leaf, head),
            P(leaf, head),
            P(leaf, None),
            P(None, head),
            P(None, head),
            P(None, head),
            P(head, None),
            P(),
        ),
        out_specs=(
            P(leaf, head),
            P(leaf, head),
            P(leaf, head),
            P(leaf, head),
            P(head, leaf),
        ),
        check_vma=False,
    )
```

```python
import functools
import math

import jax
import jax.numpy as jnp
from jax import lax
from jax.experimental import pallas as pl
from jax.experimental.pallas import tpu as pltpu
from jax.sharding import Mesh, PartitionSpec as P

HEAD_WIDTH = 128
BLOCK = 128
GROUP = 2
NZ, NY = 8, 4
DEV_BLOCKS = 3
ROW_BLOCKS = NY * DEV_BLOCKS
COL_BLOCKS = NZ * DEV_BLOCKS
PATH = 16
PAIR = GROUP * BLOCK
SCALE = HEAD_WIDTH ** (-0.5)
SCALE2 = SCALE * math.log2(math.e)
NEG = -1e30
STAT_ROWS = 16
SLOTS = 2
UNROLL = 2
GROUPS = 128
AT, SLOT, REACH, COUNT = 0, GROUPS, (1 + SLOTS) * GROUPS, (1 + 2 * SLOTS) * GROUPS
PLAN = COUNT + 128
VMEM_LIMIT = 48 * 1024 * 1024

f32 = jnp.float32
bf16 = jnp.bfloat16


def dot_nt(a, b):
    return lax.dot_general(a, b, (((1,), (1,)), ((), ())), preferred_element_type=f32)


def dot_nn(a, b):
    return jnp.dot(a, b, preferred_element_type=f32)


def prep_kernel(pos_ref, anc_ref, qd0, qd1, qd2, qd3, q_ref, d_ref, plan_ref):
    z, y = pos_ref[0], pos_ref[1]
    for s, qd in enumerate((qd0, qd1, qd2, qd3)):
        for r in range(DEV_BLOCKS):
            at = lax.rem(y - s + NY, NY) * DEV_BLOCKS + r
            rows = slice(r * BLOCK, (r + 1) * BLOCK)
            for h in range(GROUP):
                put = slice(h * BLOCK, (h + 1) * BLOCK)
                q_ref[at, put, :] = qd[rows, h * HEAD_WIDTH : (h + 1) * HEAD_WIDTH]
                d_ref[at, put, :] = qd[rows, PAIR + h * HEAD_WIDTH : PAIR + (h + 1) * HEAD_WIDTH]

    def close(group):
        for k in range(SLOTS):
            plan_ref[SLOT + k * GROUPS + group] = 0
            plan_ref[REACH + k * GROUPS + group] = -BLOCK
        plan_ref[AT + group] = 0

    def one_block(at, first):
        block = z * ROW_BLOCKS + at

        def one_key(j, count):
            c = anc_ref[block, j]
            hit = jnp.logical_and(c >= 0, lax.rem(lax.div(c, DEV_BLOCKS), NY) == y)
            group = first + lax.div(count, SLOTS)
            k = lax.rem(count, SLOTS)

            @pl.when(hit)
            def _():
                @pl.when(k == 0)
                def _():
                    close(group)
                    plan_ref[AT + group] = at

                slot = lax.div(c, ROW_BLOCKS) * DEV_BLOCKS + lax.rem(c, DEV_BLOCKS)
                plan_ref[SLOT + k * GROUPS + group] = slot
                plan_ref[REACH + k * GROUPS + group] = jnp.where(c == block, 0, BLOCK)

            return count + hit.astype(jnp.int32)

        count = lax.fori_loop(0, PATH, one_key, jnp.int32(0))
        return first + lax.div(count + SLOTS - 1, SLOTS)

    groups = lax.fori_loop(0, ROW_BLOCKS, one_block, jnp.int32(0))
    for u in range(UNROLL):
        close(groups + u)
    plan_ref[COUNT] = groups


def group_of(plan_ref, g):
    at = plan_ref[AT + g]
    slots = [plan_ref[SLOT + k * GROUPS + g] for k in range(SLOTS)]
    reach = [plan_ref[REACH + k * GROUPS + g] for k in range(SLOTS)]
    return at, slots, reach


def base2_scores(kv_ref, q, slots, reach):
    keys = jnp.concatenate([kv_ref[s, :, :HEAD_WIDTH] for s in slots], axis=0)
    s = dot_nt(keys, q) * SCALE2
    key_at = lax.broadcasted_iota(jnp.int32, (BLOCK, PAIR), 0)
    query_at = lax.rem(lax.broadcasted_iota(jnp.int32, (BLOCK, PAIR), 1), BLOCK)
    behind = key_at - query_at
    hide = jnp.concatenate([behind > r for r in reach], axis=0)
    return jnp.where(hide, NEG, s)


def value_dot(kv_ref, d, slots):
    return dot_nt(jnp.concatenate([kv_ref[s, :, HEAD_WIDTH:] for s in slots], axis=0), d)


def stats_kernel(plan_ref, kv_ref, q_ref, d_ref, out_ref):
    out_ref[0:STAT_ROWS, :] = jnp.full((STAT_ROWS, PAIR), NEG, f32)
    out_ref[STAT_ROWS:, :] = jnp.zeros((2 * STAT_ROWS, PAIR), f32)

    def step(i, _):
        done = []
        for u in range(UNROLL):
            at, slots, reach = group_of(plan_ref, i * UNROLL + u)
            s = base2_scores(kv_ref, q_ref[at], slots, reach)
            g = value_dot(kv_ref, d_ref[at], slots)
            m = jnp.max(s, axis=0, keepdims=True)
            p = jnp.exp2(s - m)
            done.append((at, m, jnp.sum(p, axis=0, keepdims=True), jnp.sum(p * g, axis=0, keepdims=True)))
        for at, m, total, dsum in done:
            rows = [pl.ds(n * STAT_ROWS + at, 1) for n in range(3)]
            before = out_ref[rows[0], :]
            top = jnp.maximum(before, m)
            old, new = jnp.exp2(before - top), jnp.exp2(m - top)
            out_ref[rows[0], :] = top
            out_ref[rows[1], :] = out_ref[rows[1], :] * old + total * new
            out_ref[rows[2], :] = out_ref[rows[2], :] * old + dsum * new
        return 0

    lax.fori_loop(0, lax.div(plan_ref[COUNT] + UNROLL - 1, UNROLL), step, 0)


def grads_kernel(
    pos_ref, plan_ref, kv_ref, kvt_ref, q_ref, d_ref, st0, st1, st2, st3,
    row_ref, col_ref,
    o_scr, dq_scr, dk_scr, dv_scr, lse_scr, delta_scr,
):
    y = pos_ref[1]
    for scr in (o_scr, dq_scr, dk_scr, dv_scr):
        def clear(i, _, scr=scr):
            scr[i] = jnp.zeros(scr.shape[1:], f32)
            return 0

        lax.fori_loop(0, scr.shape[0], clear, 0)

    tops = [st[0:STAT_ROWS, :] for st in (st0, st1, st2, st3)]
    m = functools.reduce(jnp.maximum, tops)
    factors = [jnp.exp2(t - m) for t in tops]
    total, dsum = (
        sum(st[n * STAT_ROWS : (n + 1) * STAT_ROWS, :] * f for st, f in zip((st0, st1, st2, st3), factors))
        for n in (1, 2)
    )
    lse_scr[...] = m + jnp.log2(total)
    delta_scr[...] = dsum / total

    def step(i, _):
        done = []
        for u in range(UNROLL):
            at, slots, reach = group_of(plan_ref, i * UNROLL + u)
            q, d = q_ref[at], d_ref[at]
            w = jnp.exp2(base2_scores(kv_ref, q, slots, reach) - lse_scr[pl.ds(at, 1), :])
            g = value_dot(kv_ref, d, slots)
            p = w.astype(bf16)
            ds = (w * (g - delta_scr[pl.ds(at, 1), :]) * SCALE).astype(bf16)
            kt = jnp.concatenate([kvt_ref[s, :HEAD_WIDTH, :] for s in slots], axis=1)
            vt = jnp.concatenate([kvt_ref[s, HEAD_WIDTH:, :] for s in slots], axis=1)
            done.append((at, slots, dot_nn(vt, p), dot_nn(kt, ds), dot_nn(ds, q), dot_nn(p, d)))
        for at, slots, o, dq, dk, dv in done:
            o_scr[at] += o
            dq_scr[at] += dq
            for k, slot in enumerate(slots):
                dk_scr[slot] += dk[k * BLOCK : (k + 1) * BLOCK]
                dv_scr[slot] += dv[k * BLOCK : (k + 1) * BLOCK]
        return 0

    lax.fori_loop(0, lax.div(plan_ref[COUNT] + UNROLL - 1, UNROLL), step, 0)

    def finish_row(t, _):
        for r in range(DEV_BLOCKS):
            at = lax.rem(y + t, NY) * DEV_BLOCKS + r
            cols = slice(r * BLOCK, (r + 1) * BLOCK)
            for h in range(GROUP):
                heads = slice(h * BLOCK, (h + 1) * BLOCK)
                rows = slice(h * HEAD_WIDTH, (h + 1) * HEAD_WIDTH)
                drows = slice(PAIR + h * HEAD_WIDTH, PAIR + (h + 1) * HEAD_WIDTH)
                row_ref[t, rows, cols] = o_scr[at, :, heads].astype(bf16)
                row_ref[t, drows, cols] = dq_scr[at, :, heads].astype(bf16)
        return 0

    lax.fori_loop(0, NY, finish_row, 0)

    def finish_col(c, _):
        col_ref[c, :, :HEAD_WIDTH] = dk_scr[c].astype(bf16)
        col_ref[c, :, HEAD_WIDTH:] = dv_scr[c].astype(bf16)
        return 0

    lax.fori_loop(0, COL_BLOCKS, finish_col, 0)


SMEM_SPEC = pl.BlockSpec(memory_space=pltpu.SMEM)
VMEM_SPEC = pl.BlockSpec(memory_space=pltpu.VMEM)
PARAMS = pltpu.CompilerParams(vmem_limit_bytes=VMEM_LIMIT)
STACK = jax.ShapeDtypeStruct((ROW_BLOCKS, PAIR, HEAD_WIDTH), bf16)


def prep_call(pos, anc, qds):
    return pl.pallas_call(
        prep_kernel,
        out_shape=(STACK, STACK, jax.ShapeDtypeStruct((PLAN,), jnp.int32)),
        in_specs=[SMEM_SPEC] * 2 + [VMEM_SPEC] * NY,
        out_specs=(VMEM_SPEC, VMEM_SPEC, SMEM_SPEC),
        compiler_params=PARAMS,
        name="prep",
    )(pos, anc, *qds)


def stats_call(plan, kv, q, d):
    return pl.pallas_call(
        stats_kernel,
        out_shape=jax.ShapeDtypeStruct((3 * STAT_ROWS, PAIR), f32),
        in_specs=[SMEM_SPEC] + [VMEM_SPEC] * 3,
        out_specs=VMEM_SPEC,
        compiler_params=PARAMS,
        name="stats",
    )(plan, kv, q, d)


def grads_call(pos, plan, kv, kvt, q, d, stats):
    return pl.pallas_call(
        grads_kernel,
        out_shape=(
            jax.ShapeDtypeStruct((NY, 2 * PAIR, DEV_BLOCKS * BLOCK), bf16),
            jax.ShapeDtypeStruct((COL_BLOCKS, BLOCK, 2 * HEAD_WIDTH), bf16),
        ),
        in_specs=[SMEM_SPEC] * 2 + [VMEM_SPEC] * 8,
        out_specs=(VMEM_SPEC, VMEM_SPEC),
        scratch_shapes=[
            pltpu.VMEM((ROW_BLOCKS, HEAD_WIDTH, PAIR), f32),
            pltpu.VMEM((ROW_BLOCKS, HEAD_WIDTH, PAIR), f32),
            pltpu.VMEM((COL_BLOCKS, BLOCK, HEAD_WIDTH), f32),
            pltpu.VMEM((COL_BLOCKS, BLOCK, HEAD_WIDTH), f32),
            pltpu.VMEM((STAT_ROWS, PAIR), f32),
            pltpu.VMEM((STAT_ROWS, PAIR), f32),
        ],
        compiler_params=PARAMS,
        name="grads",
    )(pos, plan, kv, kvt, q, d, *stats)


def shift(x, axis, size, by):
    return lax.ppermute(x, axis, [(i, (i + by) % size) for i in range(size)])


def per_device(
    nx, nc, normed_input, queries, keys, values, grad_out, query_weight, key_weight, value_weight, output_weight, ancestors
):
    z, y = lax.axis_index("z"), lax.axis_index("y")
    x, c = lax.axis_index("x"), lax.axis_index("c")
    rows = queries.shape[0]
    model = grad_out.shape[1]
    pos = jnp.stack([z, y]).astype(jnp.int32)

    kv = jnp.concatenate([keys, values], axis=1)
    kv = lax.all_to_all(jnp.broadcast_to(kv, (NZ,) + kv.shape), "z", 0, 0, tiled=True)
    kv = kv.reshape(COL_BLOCKS, BLOCK, 2 * HEAD_WIDTH)
    attn_grad = dot_nt(grad_out, output_weight).astype(bf16)
    mine = jnp.concatenate([queries, attn_grad], axis=1)
    qds = [mine] + [shift(mine, "y", NY, s) for s in range(1, NY)]

    heads = nx * nc
    width = model // heads

    def laid_out(w):
        w = w.reshape(nx, nc, width, w.shape[1])
        w = jnp.roll(jnp.roll(w, -x, axis=0), -c, axis=1)
        return w.transpose(1, 0, 2, 3).reshape(model, w.shape[3])

    wq = laid_out(query_weight)
    wkv = laid_out(jnp.concatenate([key_weight, value_weight], axis=1))

    part_rows = model // (NZ * NY)

    def from_y(t):
        t = t.reshape(NZ, NY, part_rows, t.shape[1])
        return jnp.roll(t, -y, axis=1).transpose(1, 0, 2, 3).reshape(model, t.shape[3])

    input_t = normed_input.T
    input_y, grad_y = from_y(input_t), from_y(grad_out.T)

    q_stack, d_stack, plan = prep_call(pos, ancestors, qds)
    own = stats_call(plan, kv, q_stack, d_stack)
    stats = [own] + [shift(own, "y", NY, s) for s in range(1, NY)]
    row_part, col_part = grads_call(pos, plan, kv, jnp.swapaxes(kv, 1, 2), q_stack, d_stack, stats)

    got = [shift(row_part[s], "y", NY, s) for s in range(1, NY)]
    col_got = lax.all_to_all(col_part.reshape(NZ, rows, 2 * HEAD_WIDTH), "z", 0, 0, tiled=True)
    row_sum = sum((g.astype(f32) for g in got), row_part[0].astype(f32)).astype(bf16)
    attn_t, dq_t = row_sum[:PAIR], row_sum[PAIR:]

    qo_part = jnp.concatenate([dot_nt(input_y, dq_t).astype(bf16), dot_nt(grad_y, attn_t).astype(bf16)], axis=1)
    qo_part = qo_part.reshape(NY, model // NY, 2 * PAIR)
    qo = qo_part[0].astype(f32)
    for s in range(1, NY):
        qo = qo + shift(qo_part[s], "y", NY, s).astype(f32)
    qo = lax.all_to_all(qo.astype(bf16).reshape(NZ, part_rows, 2 * PAIR), "z", 0, 0, tiled=True)
    qo = jnp.sum(qo.astype(f32), axis=0)

    dkv = jnp.sum(col_got.astype(f32), axis=0).astype(bf16)
    kv_part = dot_nn(input_t, dkv).astype(bf16).reshape(NZ * NY, part_rows, 2 * HEAD_WIDTH)
    kv_grad = jnp.sum(lax.all_to_all(kv_part, ("z", "y"), 0, 0, tiled=True).astype(f32), axis=0)

    part = lax.dot_general(dq_t, wq, (((0,), (1,)), ((), ())), preferred_element_type=f32)
    part = part + dot_nt(dkv, wkv)
    side = nx * width
    keep = part[:, :side]
    for s in range(1, nc):
        keep = keep + shift(part[:, s * side : (s + 1) * side].astype(bf16), "c", nc, s).astype(f32)
    input_grad = keep[:, :width]
    for s in range(1, nx):
        piece = keep[:, s * width : (s + 1) * width].astype(bf16)
        input_grad = input_grad + shift(piece, "x", nx, s).astype(f32)
    input_grad = input_grad.astype(bf16)
    return (
        input_grad,
        qo[:, :PAIR],
        kv_grad[:, :HEAD_WIDTH],
        kv_grad[:, HEAD_WIDTH:],
        qo[:, PAIR:].T,
    )


def solution(mesh):
    heads = mesh.shape["head"]
    nc = 2 if heads % 2 == 0 else 1
    nx = heads // nc
    grid = Mesh(mesh.devices.reshape(NZ, NY, nx, nc), ("z", "y", "x", "c"))
    leaf, head = ("z", "y"), ("x", "c")
    return jax.shard_map(
        functools.partial(per_device, nx, nc),
        mesh=grid,
        in_specs=(
            P(leaf, None),
            P(leaf, head),
            P(leaf, head),
            P(leaf, head),
            P(leaf, None),
            P(None, head),
            P(None, head),
            P(None, head),
            P(head, None),
            P(),
        ),
        out_specs=(
            P(leaf, head),
            P(leaf, head),
            P(leaf, head),
            P(leaf, head),
            P(head, leaf),
        ),
        check_vma=False,
    )
```

```python
import functools
import math

import jax
import jax.numpy as jnp
from jax import lax
from jax.experimental import pallas as pl
from jax.experimental.pallas import tpu as pltpu
from jax.sharding import Mesh, PartitionSpec as P

HEAD_WIDTH = 128
BLOCK = 128
GROUP = 2
NZ, NY = 8, 4
DEV_BLOCKS = 3
ROW_BLOCKS = NY * DEV_BLOCKS
COL_BLOCKS = NZ * DEV_BLOCKS
PATH = 16
PAIR = GROUP * BLOCK
SCALE = HEAD_WIDTH ** (-0.5)
SCALE2 = SCALE * math.log2(math.e)
NEG = -1e30
STAT_ROWS = 16
SLOTS = 2
UNROLL = 4
ENTRIES = 256
AT, SLOT, REACH, COUNT = 0, ENTRIES, 2 * ENTRIES, 3 * ENTRIES
PLAN = COUNT + 128

f32 = jnp.float32
bf16 = jnp.bfloat16


def dot_nt(a, b):
    return lax.dot_general(a, b, (((1,), (1,)), ((), ())), preferred_element_type=f32)


def dot_nn(a, b):
    return jnp.dot(a, b, preferred_element_type=f32)


def start_copies(pairs, sems, first=0):
    copies = [pltpu.make_async_copy(src, dst, sems.at[first + i]) for i, (src, dst) in enumerate(pairs)]
    for copy in copies:
        copy.start()
    return copies


def copy_all(pairs, sems):
    for copy in start_copies(pairs, sems):
        copy.wait()


def start_kernel(query_any, key_any, value_any, grad_any, weight_any, qd_ref, kv_ref, grad_ref, weight_ref, sems):
    copies = start_copies(
        (
            (grad_any, grad_ref),
            (weight_any, weight_ref),
            (key_any, kv_ref.at[:, pl.ds(0, HEAD_WIDTH)]),
            (value_any, kv_ref.at[:, pl.ds(HEAD_WIDTH, HEAD_WIDTH)]),
            (query_any, qd_ref.at[:, pl.ds(0, PAIR)]),
        ),
        sems,
    )
    copies[0].wait()
    copies[1].wait()
    qd_ref[:, PAIR:] = dot_nt(grad_ref[...], weight_ref[...]).astype(bf16)
    for copy in copies[2:]:
        copy.wait()


def stack_kernel(own, before, after, top, bottom, out_ref, sems):
    y = lax.axis_index("y")
    pairs = []

    def put(src, src_row, back, row, count):
        at = lax.rem(y - back + NY, NY) * DEV_BLOCKS + row // BLOCK
        for k in range(2):
            for h in range(GROUP):
                src_cols = pl.ds(k * PAIR + h * HEAD_WIDTH, HEAD_WIDTH)
                dst = out_ref.at[at, pl.ds(h * BLOCK + row % BLOCK, count), pl.ds(k * HEAD_WIDTH, HEAD_WIDTH)]
                pairs.append((src.at[pl.ds(src_row, count), src_cols], dst))

    half = BLOCK // 2
    for src, back in ((own, 0), (before, 1), (after, 3)):
        for r in range(DEV_BLOCKS):
            put(src, r * BLOCK, back, r * BLOCK, BLOCK)
    put(top, 0, 2, 0, BLOCK)
    put(top, BLOCK, 2, BLOCK, half)
    put(bottom, 0, 2, BLOCK + half, half)
    put(bottom, half, 2, 2 * BLOCK, BLOCK)
    copy_all(pairs, sems)


def plan_kernel(anc_ref, plan_ref):
    z, y = lax.axis_index("z"), lax.axis_index("y")

    def put(e, at, slot, reach):
        plan_ref[AT + e] = at
        plan_ref[SLOT + e] = slot
        plan_ref[REACH + e] = reach

    def one_block(at, first):
        block = z * ROW_BLOCKS + at

        def one_key(j, e):
            c = anc_ref[j, block]
            device = lax.div(c, DEV_BLOCKS)
            row = lax.div(device, NY)
            hit = jnp.logical_and(c >= 0, device - row * NY == y)
            slot = row * DEV_BLOCKS + c - device * DEV_BLOCKS
            put(e, at, slot, jnp.where(c == block, 0, BLOCK))
            return e + hit.astype(jnp.int32)

        e = lax.fori_loop(0, PATH, one_key, first, unroll=True)
        put(e, at, 0, -BLOCK)
        return e + lax.rem(e, SLOTS)

    end = lax.fori_loop(0, ROW_BLOCKS, one_block, jnp.int32(0))
    for u in range(SLOTS * UNROLL):
        put(end + u, 0, 0, -BLOCK)
    plan_ref[COUNT] = lax.div(end, SLOTS)


def group_of(plan_ref, g):
    slots = [plan_ref[SLOT + SLOTS * g + k] for k in range(SLOTS)]
    reach = [plan_ref[REACH + SLOTS * g + k] for k in range(SLOTS)]
    return plan_ref[AT + SLOTS * g], slots, reach


def base2_scores(kv_ref, q, slots, reach):
    keys = jnp.concatenate([kv_ref[s, :, :HEAD_WIDTH] for s in slots], axis=0)
    s = dot_nt(keys, q) * SCALE2
    key_at = lax.broadcasted_iota(jnp.int32, (BLOCK, PAIR), 0)
    query_at = lax.rem(lax.broadcasted_iota(jnp.int32, (BLOCK, PAIR), 1), BLOCK)
    behind = key_at - query_at
    hide = jnp.concatenate([behind > r for r in reach], axis=0)
    return jnp.where(hide, NEG, s)


def value_dot(kv_ref, d, slots):
    return dot_nt(jnp.concatenate([kv_ref[s, :, HEAD_WIDTH:] for s in slots], axis=0), d)


def stats_kernel(plan_any, *refs):
    pieces, (qd_any, out_ref, kv_ref, qd_ref, plan_ref, sems) = refs[:9], refs[9:]
    z = lax.axis_index("z")

    def slots_of(back):
        return pl.ds(lax.rem(z - back + NZ, NZ) * DEV_BLOCKS, DEV_BLOCKS)

    pairs = [(qd_any, qd_ref), (plan_any, plan_ref)]
    for piece, back in zip(pieces[:7], (0, 1, 2, 3, 5, 6, 7)):
        pairs.append((piece, kv_ref.at[slots_of(back)]))
    far = lax.rem(z + NZ // 2, NZ) * DEV_BLOCKS
    half = BLOCK // 2
    pairs.append((pieces[7].at[0:1], kv_ref.at[pl.ds(far, 1)]))
    pairs.append((pieces[7].at[1, pl.ds(0, half)], kv_ref.at[far + 1, pl.ds(0, half)]))
    pairs.append((pieces[8].at[0, pl.ds(half, half)], kv_ref.at[far + 1, pl.ds(half, half)]))
    pairs.append((pieces[8].at[1:2], kv_ref.at[pl.ds(far + 2, 1)]))
    copy_all(pairs, sems)
    out_ref[0:STAT_ROWS, :] = jnp.full((STAT_ROWS, PAIR), NEG, f32)
    out_ref[STAT_ROWS:, :] = jnp.zeros((2 * STAT_ROWS, PAIR), f32)

    def step(i, _):
        done = []
        for u in range(UNROLL):
            at, slots, reach = group_of(plan_ref, i * UNROLL + u)
            s = base2_scores(kv_ref, qd_ref[at, :, :HEAD_WIDTH], slots, reach)
            g = value_dot(kv_ref, qd_ref[at, :, HEAD_WIDTH:], slots)
            m = jnp.max(s, axis=0, keepdims=True)
            p = jnp.exp2(s - m)
            done.append((at, m, jnp.sum(p, axis=0, keepdims=True), jnp.sum(p * g, axis=0, keepdims=True)))
        for at, m, total, dsum in done:
            rows = [pl.ds(n * STAT_ROWS + at, 1) for n in range(3)]
            before = out_ref[rows[0], :]
            top = jnp.maximum(before, m)
            old, new = jnp.exp2(before - top), jnp.exp2(m - top)
            out_ref[rows[0], :] = top
            out_ref[rows[1], :] = out_ref[rows[1], :] * old + total * new
            out_ref[rows[2], :] = out_ref[rows[2], :] * old + dsum * new
        return 0

    lax.fori_loop(0, lax.div(plan_ref[COUNT] + UNROLL - 1, UNROLL), step, 0)


def grads_kernel(
    plan_any, kv_any, kvt_any, qd_any, st0, st1, st2, st3,
    row0, row1, row2, row3, col_any,
    o_scr, dq_scr, dk_scr, dv_scr, lse_scr, delta_scr,
    kv_ref, kvt_ref, qd_ref, plan_ref, row_scr, col_scr, sems,
):
    y = lax.axis_index("y")
    pairs = ((kv_any, kv_ref), (kvt_any, kvt_ref), (qd_any, qd_ref), (plan_any, plan_ref))
    copies = start_copies(pairs, sems)
    for scr in (o_scr, dq_scr, dk_scr, dv_scr):
        def clear(i, _, scr=scr):
            scr[i] = jnp.zeros(scr.shape[1:], f32)
            return 0

        lax.fori_loop(0, scr.shape[0], clear, 0)

    tops = [st[0:STAT_ROWS, :] for st in (st0, st1, st2, st3)]
    m = functools.reduce(jnp.maximum, tops)
    factors = [jnp.exp2(t - m) for t in tops]
    total, dsum = (
        sum(st[n * STAT_ROWS : (n + 1) * STAT_ROWS, :] * f for st, f in zip((st0, st1, st2, st3), factors))
        for n in (1, 2)
    )
    lse_scr[...] = m + jnp.log2(total)
    delta_scr[...] = dsum / total
    for copy in copies:
        copy.wait()

    def step(i, _):
        done = []
        for u in range(UNROLL):
            at, slots, reach = group_of(plan_ref, i * UNROLL + u)
            q, d = qd_ref[at, :, :HEAD_WIDTH], qd_ref[at, :, HEAD_WIDTH:]
            w = jnp.exp2(base2_scores(kv_ref, q, slots, reach) - lse_scr[pl.ds(at, 1), :])
            g = value_dot(kv_ref, d, slots)
            p = w.astype(bf16)
            ds = (w * (g - delta_scr[pl.ds(at, 1), :]) * SCALE).astype(bf16)
            kt = jnp.concatenate([kvt_ref[s, :HEAD_WIDTH, :] for s in slots], axis=1)
            vt = jnp.concatenate([kvt_ref[s, HEAD_WIDTH:, :] for s in slots], axis=1)
            done.append((at, slots, dot_nn(vt, p), dot_nn(kt, ds), dot_nn(ds, q), dot_nn(p, d)))
        for at, slots, o, dq, dk, dv in done:
            o_scr[at] += o
            dq_scr[at] += dq
            for k, slot in enumerate(slots):
                dk_scr[slot] += dk[k * BLOCK : (k + 1) * BLOCK]
                dv_scr[slot] += dv[k * BLOCK : (k + 1) * BLOCK]
        return 0

    lax.fori_loop(0, lax.div(plan_ref[COUNT] + UNROLL - 1, UNROLL), step, 0)

    copies = []
    for n in range(NZ):
        for c in range(n * DEV_BLOCKS, (n + 1) * DEV_BLOCKS):
            col_scr[c, :, :HEAD_WIDTH] = dk_scr[c].astype(bf16)
            col_scr[c, :, HEAD_WIDTH:] = dv_scr[c].astype(bf16)
        part = pl.ds(n * DEV_BLOCKS, DEV_BLOCKS)
        copies += start_copies([(col_scr.at[part], col_any.at[part])], sems, 4 + n)
    for t, row_ref in enumerate((row0, row1, row2, row3)):
        for r in range(DEV_BLOCKS):
            at = lax.rem(y + t, NY) * DEV_BLOCKS + r
            cols = slice(r * BLOCK, (r + 1) * BLOCK)
            for h in range(GROUP):
                heads = slice(h * BLOCK, (h + 1) * BLOCK)
                rows = slice(h * HEAD_WIDTH, (h + 1) * HEAD_WIDTH)
                drows = slice(PAIR + h * HEAD_WIDTH, PAIR + (h + 1) * HEAD_WIDTH)
                row_scr[t, rows, cols] = o_scr[at, :, heads].astype(bf16)
                row_scr[t, drows, cols] = dq_scr[at, :, heads].astype(bf16)
        copies += start_copies([(row_scr.at[t], row_ref)], sems, 4 + NZ + t)
    for copy in copies:
        copy.wait()


def turn_kernel(kv_ref, out_ref):
    def one(c, _):
        for k in range(2):
            cols = slice(k * HEAD_WIDTH, (k + 1) * HEAD_WIDTH)
            out_ref[c, cols, :] = kv_ref[c, :, cols].T
        return 0

    lax.fori_loop(0, COL_BLOCKS, one, 0, unroll=4)


def scatter_rows(part_ref, cols, value):
    y = lax.axis_index("y")
    step = value.shape[0] // (NZ * NY)
    value = value.astype(bf16)
    for i in range(NZ * NY):
        n, t = divmod(i, NY)
        part_ref[lax.rem(t - y + NY, NY), n * step : (n + 1) * step, cols] = value[i * step : (i + 1) * step]


def model_rows(i, nx, nc, width):
    head = lax.rem(lax.axis_index("x") + i % nx, nx) * nc + lax.rem(lax.axis_index("c") + i // nx, nc)
    return pl.ds(pl.multiple_of(head * width, width), width)


def rows_kernel(
    nx, nc, row0, row1, row2, row3, input_any, grad_any, wq_any, part_any, back_any, turned_any,
    got, input_ref, grad_ref, wq_ref, part_ref, back_ref, turned_ref, sems,
):
    pairs = [(row, got.at[t]) for t, row in enumerate((row0, row1, row2, row3))]
    pairs += [(input_any, input_ref), (grad_any, grad_ref), (wq_any, wq_ref)]
    copies = start_copies(pairs, sems)
    for copy in copies:
        copy.wait()
    turned_ref[...] = input_ref[...].T
    copies = start_copies([(turned_ref, turned_any)], sems, 7)
    o = sum(got[t, :PAIR, :].astype(f32) for t in range(NY)).astype(bf16)
    dq = sum(got[t, PAIR:, :].astype(f32) for t in range(NY)).astype(bf16)
    scatter_rows(part_ref, slice(0, PAIR), dot_nt(turned_ref[...], dq))
    scatter_rows(part_ref, slice(PAIR, 2 * PAIR), dot_nt(grad_ref[...].T, o))
    copies += start_copies([(part_ref, part_any)], sems, 8)
    width = wq_ref.shape[0] // (nx * nc)
    for i in range(nx * nc):
        back_ref[i * width : (i + 1) * width, :] = dot_nn(wq_ref[model_rows(i, nx, nc, width), :], dq)
    copies += start_copies([(back_ref, back_any)], sems, 9)
    for copy in copies:
        copy.wait()


def cols_kernel(
    nx, nc, got_any, turned_any, wk_any, wv_any, back_any, part_ref, send_ref, keep_ref,
    got_ref, turned_ref, wk_ref, wv_ref, back_ref, sems,
):
    pairs = [(got_any, got_ref), (turned_any, turned_ref), (wk_any, wk_ref), (wv_any, wv_ref), (back_any, back_ref)]
    copies = start_copies(pairs, sems)
    copies[0].wait()
    d = sum(got_ref[t].astype(f32) for t in range(NZ)).astype(bf16)
    copies[1].wait()
    scatter_rows(part_ref, slice(0, 2 * HEAD_WIDTH), dot_nn(turned_ref[...], d))
    for copy in copies[2:]:
        copy.wait()
    width = wk_ref.shape[0] // (nx * nc)
    for i in range(nx * nc):
        rows = model_rows(i, nx, nc, width)
        w = jnp.concatenate([wk_ref[rows, :], wv_ref[rows, :]], axis=1)
        part = back_ref[i * width : (i + 1) * width, :] + dot_nt(w, d)
        if i < nx:
            keep_ref[i * width : (i + 1) * width, :] = part
        else:
            send_ref[(i - nx) * width : (i - nx + 1) * width, :] = part.astype(bf16)


SMEM_SPEC = pl.BlockSpec(memory_space=pltpu.SMEM)
VMEM_SPEC = pl.BlockSpec(memory_space=pltpu.VMEM)
HBM_SPEC = pl.BlockSpec(memory_space=pltpu.HBM)


def vmem(mib):
    return pltpu.CompilerParams(vmem_limit_bytes=mib * 1024 * 1024)


STACK = jax.ShapeDtypeStruct((ROW_BLOCKS, PAIR, 2 * HEAD_WIDTH), bf16)


def start_call(queries, keys, values, grad_out, output_weight):
    tokens = queries.shape[0]
    return pl.pallas_call(
        start_kernel,
        out_shape=(
            jax.ShapeDtypeStruct((tokens, 2 * PAIR), bf16),
            jax.ShapeDtypeStruct((tokens, 2 * HEAD_WIDTH), bf16),
        ),
        in_specs=[HBM_SPEC] * 5,
        out_specs=(VMEM_SPEC,) * 2,
        scratch_shapes=[
            pltpu.VMEM(grad_out.shape, bf16),
            pltpu.VMEM(output_weight.shape, bf16),
            pltpu.SemaphoreType.DMA((5,)),
        ],
        compiler_params=vmem(54),
        name="start",
    )(queries, keys, values, grad_out, output_weight)


def plan_call(anc):
    return pl.pallas_call(
        plan_kernel,
        out_shape=jax.ShapeDtypeStruct((PLAN,), jnp.int32),
        in_specs=[SMEM_SPEC],
        out_specs=SMEM_SPEC,
        name="plan",
    )(anc)


def stack_call(qds):
    return pl.pallas_call(
        stack_kernel,
        out_shape=STACK,
        in_specs=[HBM_SPEC] * 5,
        out_specs=HBM_SPEC,
        scratch_shapes=[pltpu.SemaphoreType.DMA((2 * GROUP * (3 * DEV_BLOCKS + 4),))],
        compiler_params=vmem(4),
        name="stack",
    )(*qds)


def stats_call(plan, pieces, qd):
    return pl.pallas_call(
        stats_kernel,
        out_shape=(
            jax.ShapeDtypeStruct((3 * STAT_ROWS, PAIR), f32),
            jax.ShapeDtypeStruct((COL_BLOCKS, BLOCK, 2 * HEAD_WIDTH), bf16),
        ),
        in_specs=[HBM_SPEC] * 11,
        out_specs=(VMEM_SPEC, VMEM_SPEC),
        scratch_shapes=[
            pltpu.VMEM(STACK.shape, bf16),
            pltpu.SMEM((PLAN,), jnp.int32),
            pltpu.SemaphoreType.DMA((13,)),
        ],
        compiler_params=vmem(12),
        name="stats",
    )(plan, *pieces, qd)


def grads_call(plan, kv, kvt, qd, stats):
    return pl.pallas_call(
        grads_kernel,
        out_shape=(
            *[jax.ShapeDtypeStruct((2 * PAIR, DEV_BLOCKS * BLOCK), bf16)] * NY,
            jax.ShapeDtypeStruct((COL_BLOCKS, BLOCK, 2 * HEAD_WIDTH), bf16),
        ),
        in_specs=[HBM_SPEC] * 4 + [VMEM_SPEC] * 4,
        out_specs=(HBM_SPEC,) * 5,
        scratch_shapes=[
            pltpu.VMEM((ROW_BLOCKS, HEAD_WIDTH, PAIR), f32),
            pltpu.VMEM((ROW_BLOCKS, HEAD_WIDTH, PAIR), f32),
            pltpu.VMEM((COL_BLOCKS, BLOCK, HEAD_WIDTH), f32),
            pltpu.VMEM((COL_BLOCKS, BLOCK, HEAD_WIDTH), f32),
            pltpu.VMEM((STAT_ROWS, PAIR), f32),
            pltpu.VMEM((STAT_ROWS, PAIR), f32),
            pltpu.VMEM((COL_BLOCKS, BLOCK, 2 * HEAD_WIDTH), bf16),
            pltpu.VMEM((COL_BLOCKS, 2 * HEAD_WIDTH, BLOCK), bf16),
            pltpu.VMEM(STACK.shape, bf16),
            pltpu.SMEM((PLAN,), jnp.int32),
            pltpu.VMEM((NY, 2 * PAIR, DEV_BLOCKS * BLOCK), bf16),
            pltpu.VMEM((COL_BLOCKS, BLOCK, 2 * HEAD_WIDTH), bf16),
            pltpu.SemaphoreType.DMA((4 + NZ + NY,)),
        ],
        compiler_params=vmem(54),
        name="grads",
    )(plan, kv, kvt, qd, *stats)


def turn_call(kv):
    return pl.pallas_call(
        turn_kernel,
        out_shape=jax.ShapeDtypeStruct((COL_BLOCKS, 2 * HEAD_WIDTH, BLOCK), bf16),
        in_specs=[VMEM_SPEC],
        out_specs=VMEM_SPEC,
        compiler_params=vmem(8),
        name="turn",
    )(kv)


def shift(x, axis, size, by):
    return lax.ppermute(x, axis, [(i, (i + by) % size) for i in range(size)])


def rows_call(nx, nc, got, normed_input, grad_out, query_weight):
    tokens, model = normed_input.shape
    return pl.pallas_call(
        functools.partial(rows_kernel, nx, nc),
        out_shape=(
            jax.ShapeDtypeStruct((NY, model // NY, 2 * PAIR), bf16),
            jax.ShapeDtypeStruct((model, tokens), f32),
            jax.ShapeDtypeStruct((model, tokens), bf16),
        ),
        in_specs=[HBM_SPEC] * 7,
        out_specs=(HBM_SPEC,) * 3,
        scratch_shapes=[
            pltpu.VMEM((NY, 2 * PAIR, tokens), bf16),
            pltpu.VMEM(normed_input.shape, bf16),
            pltpu.VMEM(normed_input.shape, bf16),
            pltpu.VMEM(query_weight.shape, bf16),
            pltpu.VMEM((NY, model // NY, 2 * PAIR), bf16),
            pltpu.VMEM((model, tokens), f32),
            pltpu.VMEM((model, tokens), bf16),
            pltpu.SemaphoreType.DMA((10,)),
        ],
        compiler_params=vmem(54),
        name="rows",
    )(*got, normed_input, grad_out, query_weight)


def cols_call(nx, nc, got, turned, key_weight, value_weight, back):
    model, tokens = turned.shape
    side = model // nc
    return pl.pallas_call(
        functools.partial(cols_kernel, nx, nc),
        out_shape=(
            jax.ShapeDtypeStruct((NY, model // NY, 2 * HEAD_WIDTH), bf16),
            jax.ShapeDtypeStruct((max(model - side, side), tokens), bf16),
            jax.ShapeDtypeStruct((side, tokens), f32),
        ),
        in_specs=[HBM_SPEC] * 5,
        out_specs=(VMEM_SPEC,) * 3,
        scratch_shapes=[
            pltpu.VMEM(got.shape, bf16),
            pltpu.VMEM(turned.shape, bf16),
            pltpu.VMEM(key_weight.shape, bf16),
            pltpu.VMEM(value_weight.shape, bf16),
            pltpu.VMEM(back.shape, f32),
            pltpu.SemaphoreType.DMA((5,)),
        ],
        compiler_params=vmem(20),
        name="cols",
    )(got, turned, key_weight, value_weight, back)


def ring_gather(own):
    up, down = [own], [own]
    for _ in range(3):
        up.append(shift(up[-1], "z", NZ, 1))
        down.append(shift(down[-1], "z", NZ, -1))
    pieces = [p.reshape(DEV_BLOCKS, BLOCK, 2 * HEAD_WIDTH) for p in up + down[:0:-1]]
    top = shift(up[-1][: 2 * BLOCK], "z", NZ, 1)
    bottom = shift(down[-1][BLOCK:], "z", NZ, -1)
    return pieces + [top.reshape(2, BLOCK, 2 * HEAD_WIDTH), bottom.reshape(2, BLOCK, 2 * HEAD_WIDTH)]


def per_device(
    nx, nc, normed_input, queries, keys, values, grad_out, query_weight, key_weight, value_weight, output_weight, ancestors
):
    model = grad_out.shape[1]

    mine, kv = start_call(queries, keys, values, grad_out, output_weight)
    pieces = ring_gather(kv)
    before, after = shift(mine, "y", NY, 1), shift(mine, "y", NY, -1)
    half = mine.shape[0] // 2
    qds = [mine, before, after, shift(before[:half], "y", NY, 1), shift(after[half:], "y", NY, -1)]

    plan = plan_call(ancestors.T)
    qd = stack_call(qds)
    own, kv = stats_call(plan, pieces, qd)
    stats = [own] + [shift(own, "y", NY, s) for s in range(1, NY)]
    *row_part, col_part = grads_call(plan, kv, turn_call(kv), qd, stats)

    col_got = lax.all_to_all(col_part.reshape(NZ, DEV_BLOCKS * BLOCK, 2 * HEAD_WIDTH), "z", 0, 0, tiled=True)
    row_got = [row_part[0]] + [shift(row_part[s], "y", NY, s) for s in range(1, NY)]

    part_rows = model // (NZ * NY)
    qo_part, back, turned = rows_call(nx, nc, row_got, normed_input, grad_out, query_weight)
    qo_got = [qo_part[0]] + [shift(qo_part[s], "y", NY, s) for s in range(1, NY)]

    kv_part, send, keep = cols_call(nx, nc, col_got, turned, key_weight, value_weight, back)
    kv_got = [kv_part[0]] + [shift(kv_part[s], "y", NY, s) for s in range(1, NY)]
    sums = [sum(g.astype(f32) for g in got).astype(bf16) for got in (qo_got, kv_got)]
    sums = jnp.concatenate(sums, axis=1).reshape(NZ, part_rows, 2 * PAIR + 2 * HEAD_WIDTH)
    sums = jnp.sum(lax.all_to_all(sums, "z", 0, 0, tiled=True).astype(f32), axis=0)

    width = model // (nx * nc)
    side = nx * width
    for s in range(1, nc):
        keep = keep + shift(send[(s - 1) * side : s * side], "c", nc, s).astype(f32)
    input_grad = keep[:width]
    for s in range(1, nx):
        piece = keep[s * width : (s + 1) * width].astype(bf16)
        input_grad = input_grad + shift(piece, "x", nx, s).astype(f32)
    return (
        input_grad.astype(bf16).T,
        sums[:, :PAIR],
        sums[:, 2 * PAIR : 2 * PAIR + HEAD_WIDTH],
        sums[:, 2 * PAIR + HEAD_WIDTH :],
        sums[:, PAIR : 2 * PAIR].T,
    )


def solution(mesh):
    heads = mesh.shape["head"]
    nc = 2 if heads % 2 == 0 else 1
    nx = heads // nc
    grid = Mesh(mesh.devices.reshape(NZ, NY, nx, nc), ("z", "y", "x", "c"))
    leaf, head = ("z", "y"), ("x", "c")
    return jax.shard_map(
        functools.partial(per_device, nx, nc),
        mesh=grid,
        in_specs=(
            P(leaf, None),
            P(leaf, head),
            P(leaf, head),
            P(leaf, head),
            P(leaf, None),
            P(None, head),
            P(None, head),
            P(None, head),
            P(head, None),
            P(),
        ),
        out_specs=(
            P(leaf, head),
            P(leaf, head),
            P(leaf, head),
            P(leaf, head),
            P(head, leaf),
        ),
        check_vma=False,
    )
```

```python
import functools
import math

import jax
import jax.numpy as jnp
from jax import lax
from jax.experimental import pallas as pl
from jax.experimental.pallas import tpu as pltpu
from jax.sharding import Mesh, PartitionSpec as P

HEAD_WIDTH = 128
BLOCK = 128
GROUP = 2
NZ, NY = 8, 4
DEV_BLOCKS = 3
ROW_BLOCKS = NY * DEV_BLOCKS
COL_BLOCKS = NZ * DEV_BLOCKS
PATH = 16
PAIR = GROUP * BLOCK
SCALE = HEAD_WIDTH ** (-0.5)
SCALE2 = SCALE * math.log2(math.e)
NEG = -1e30
STAT_ROWS = 16
SLOTS = 2
UNROLL = 4
ENTRIES = 256
AT, SLOT, REACH, COUNT = 0, ENTRIES, 2 * ENTRIES, 3 * ENTRIES
PLAN = COUNT + 128

f32 = jnp.float32
bf16 = jnp.bfloat16


def dot_nt(a, b):
    return lax.dot_general(a, b, (((1,), (1,)), ((), ())), preferred_element_type=f32)


def dot_nn(a, b):
    return jnp.dot(a, b, preferred_element_type=f32)


def start_copies(pairs, sems, first=0):
    copies = [pltpu.make_async_copy(src, dst, sems.at[first + i]) for i, (src, dst) in enumerate(pairs)]
    for copy in copies:
        copy.start()
    return copies


def copy_all(pairs, sems):
    for copy in start_copies(pairs, sems):
        copy.wait()


def join_kernel(key_any, value_any, kv_ref, sems):
    copy_all(
        (
            (key_any, kv_ref.at[:, pl.ds(0, HEAD_WIDTH)]),
            (value_any, kv_ref.at[:, pl.ds(HEAD_WIDTH, HEAD_WIDTH)]),
        ),
        sems,
    )


def start_kernel(query_any, grad_any, weight_any, qd_ref, grad_ref, weight_ref, sems):
    pairs = ((grad_any, grad_ref), (weight_any, weight_ref), (query_any, qd_ref.at[:, pl.ds(0, PAIR)]))
    copies = start_copies(pairs, sems)
    copies[0].wait()
    copies[1].wait()
    qd_ref[:, PAIR:] = dot_nt(grad_ref[...], weight_ref[...]).astype(bf16)
    copies[2].wait()


def stack_kernel(own, before, after, top, bottom, out_ref, sems):
    y = lax.axis_index("y")
    pairs = []

    def put(src, src_row, back, row, count):
        at = lax.rem(y - back + NY, NY) * DEV_BLOCKS + row // BLOCK
        for k in range(2):
            for h in range(GROUP):
                src_cols = pl.ds(k * PAIR + h * HEAD_WIDTH, HEAD_WIDTH)
                dst = out_ref.at[at, pl.ds(h * BLOCK + row % BLOCK, count), pl.ds(k * HEAD_WIDTH, HEAD_WIDTH)]
                pairs.append((src.at[pl.ds(src_row, count), src_cols], dst))

    half = BLOCK // 2
    for src, back in ((own, 0), (before, 1), (after, 3)):
        for r in range(DEV_BLOCKS):
            put(src, r * BLOCK, back, r * BLOCK, BLOCK)
    put(top, 0, 2, 0, BLOCK)
    put(top, BLOCK, 2, BLOCK, half)
    put(bottom, 0, 2, BLOCK + half, half)
    put(bottom, half, 2, 2 * BLOCK, BLOCK)
    copy_all(pairs, sems)


def plan_kernel(anc_ref, plan_ref):
    z, y = lax.axis_index("z"), lax.axis_index("y")

    def put(e, at, slot, reach):
        plan_ref[AT + e] = at
        plan_ref[SLOT + e] = slot
        plan_ref[REACH + e] = reach

    def one_block(at, first):
        block = z * ROW_BLOCKS + at

        def one_key(j, e):
            c = anc_ref[j, block]
            device = lax.div(c, DEV_BLOCKS)
            row = lax.div(device, NY)
            hit = jnp.logical_and(c >= 0, device - row * NY == y)
            slot = row * DEV_BLOCKS + c - device * DEV_BLOCKS
            put(e, at, slot, jnp.where(c == block, 0, BLOCK))
            return e + hit.astype(jnp.int32)

        e = lax.fori_loop(0, PATH, one_key, first, unroll=True)
        put(e, at, 0, -BLOCK)
        return e + lax.rem(e, SLOTS)

    end = lax.fori_loop(0, ROW_BLOCKS, one_block, jnp.int32(0))
    for u in range(SLOTS * UNROLL):
        put(end + u, 0, 0, -BLOCK)
    plan_ref[COUNT] = lax.div(end, SLOTS)


def group_of(plan_ref, g):
    slots = [plan_ref[SLOT + SLOTS * g + k] for k in range(SLOTS)]
    reach = [plan_ref[REACH + SLOTS * g + k] for k in range(SLOTS)]
    return plan_ref[AT + SLOTS * g], slots, reach


def base2_scores(kv_ref, q, slots, reach):
    keys = jnp.concatenate([kv_ref[s, :, :HEAD_WIDTH] for s in slots], axis=0)
    s = dot_nt(keys, q) * SCALE2
    key_at = lax.broadcasted_iota(jnp.int32, (BLOCK, PAIR), 0)
    query_at = lax.rem(lax.broadcasted_iota(jnp.int32, (BLOCK, PAIR), 1), BLOCK)
    behind = key_at - query_at
    hide = jnp.concatenate([behind > r for r in reach], axis=0)
    return jnp.where(hide, NEG, s)


def value_dot(kv_ref, d, slots):
    return dot_nt(jnp.concatenate([kv_ref[s, :, HEAD_WIDTH:] for s in slots], axis=0), d)


def stats_kernel(plan_any, *refs):
    pieces, (qd_ref, out_ref, kv_ref, plan_ref, sems) = refs[:9], refs[9:]
    z = lax.axis_index("z")

    def slots_of(back):
        return pl.ds(lax.rem(z - back + NZ, NZ) * DEV_BLOCKS, DEV_BLOCKS)

    pairs = [(plan_any, plan_ref)]
    for piece, back in zip(pieces[:7], (0, 1, 2, 3, 5, 6, 7)):
        pairs.append((piece, kv_ref.at[slots_of(back)]))
    far = lax.rem(z + NZ // 2, NZ) * DEV_BLOCKS
    half = BLOCK // 2
    pairs.append((pieces[7].at[0:1], kv_ref.at[pl.ds(far, 1)]))
    pairs.append((pieces[7].at[1, pl.ds(0, half)], kv_ref.at[far + 1, pl.ds(0, half)]))
    pairs.append((pieces[8].at[0, pl.ds(half, half)], kv_ref.at[far + 1, pl.ds(half, half)]))
    pairs.append((pieces[8].at[1:2], kv_ref.at[pl.ds(far + 2, 1)]))
    copy_all(pairs, sems)
    out_ref[0:STAT_ROWS, :] = jnp.full((STAT_ROWS, PAIR), NEG, f32)
    out_ref[STAT_ROWS:, :] = jnp.zeros((2 * STAT_ROWS, PAIR), f32)

    def step(i, _):
        done = []
        for u in range(UNROLL):
            at, slots, reach = group_of(plan_ref, i * UNROLL + u)
            s = base2_scores(kv_ref, qd_ref[at, :, :HEAD_WIDTH], slots, reach)
            g = value_dot(kv_ref, qd_ref[at, :, HEAD_WIDTH:], slots)
            m = jnp.max(s, axis=0, keepdims=True)
            p = jnp.exp2(s - m)
            done.append((at, m, jnp.sum(p, axis=0, keepdims=True), jnp.sum(p * g, axis=0, keepdims=True)))
        for at, m, total, dsum in done:
            rows = [pl.ds(n * STAT_ROWS + at, 1) for n in range(3)]
            before = out_ref[rows[0], :]
            top = jnp.maximum(before, m)
            old, new = jnp.exp2(before - top), jnp.exp2(m - top)
            out_ref[rows[0], :] = top
            out_ref[rows[1], :] = out_ref[rows[1], :] * old + total * new
            out_ref[rows[2], :] = out_ref[rows[2], :] * old + dsum * new
        return 0

    lax.fori_loop(0, lax.div(plan_ref[COUNT] + UNROLL - 1, UNROLL), step, 0)


def grads_kernel(
    plan_any, kv_any, qd_any, st0, st1, st2, st3,
    row0, row1, row2, row3, col_any,
    o_scr, dq_scr, dk_scr, dv_scr, lse_scr, delta_scr,
    kv_ref, kvt_ref, qd_ref, plan_ref, row_scr, col_scr, sems,
):
    y = lax.axis_index("y")
    pairs = ((kv_any, kv_ref), (qd_any, qd_ref), (plan_any, plan_ref))
    copies = start_copies(pairs, sems)
    for scr in (o_scr, dq_scr, dk_scr, dv_scr):
        def clear(i, _, scr=scr):
            scr[i] = jnp.zeros(scr.shape[1:], f32)
            return 0

        lax.fori_loop(0, scr.shape[0], clear, 0)

    tops = [st[0:STAT_ROWS, :] for st in (st0, st1, st2, st3)]
    m = functools.reduce(jnp.maximum, tops)
    factors = [jnp.exp2(t - m) for t in tops]
    total, dsum = (
        sum(st[n * STAT_ROWS : (n + 1) * STAT_ROWS, :] * f for st, f in zip((st0, st1, st2, st3), factors))
        for n in (1, 2)
    )
    lse_scr[...] = m + jnp.log2(total)
    delta_scr[...] = dsum / total
    copies[0].wait()

    def turn(c, _):
        for k in range(2):
            cols = slice(k * HEAD_WIDTH, (k + 1) * HEAD_WIDTH)
            kvt_ref[c, cols, :] = kv_ref[c, :, cols].T
        return 0

    lax.fori_loop(0, COL_BLOCKS, turn, 0, unroll=4)
    for copy in copies[1:]:
        copy.wait()

    def step(i, _):
        done = []
        for u in range(UNROLL):
            at, slots, reach = group_of(plan_ref, i * UNROLL + u)
            q, d = qd_ref[at, :, :HEAD_WIDTH], qd_ref[at, :, HEAD_WIDTH:]
            w = jnp.exp2(base2_scores(kv_ref, q, slots, reach) - lse_scr[pl.ds(at, 1), :])
            g = value_dot(kv_ref, d, slots)
            p = w.astype(bf16)
            ds = (w * (g - delta_scr[pl.ds(at, 1), :]) * SCALE).astype(bf16)
            kt = jnp.concatenate([kvt_ref[s, :HEAD_WIDTH, :] for s in slots], axis=1)
            vt = jnp.concatenate([kvt_ref[s, HEAD_WIDTH:, :] for s in slots], axis=1)
            done.append((at, slots, dot_nn(vt, p), dot_nn(kt, ds), dot_nn(ds, q), dot_nn(p, d)))
        for at, slots, o, dq, dk, dv in done:
            o_scr[at] += o
            dq_scr[at] += dq
            for k, slot in enumerate(slots):
                dk_scr[slot] += dk[k * BLOCK : (k + 1) * BLOCK]
                dv_scr[slot] += dv[k * BLOCK : (k + 1) * BLOCK]
        return 0

    lax.fori_loop(0, lax.div(plan_ref[COUNT] + UNROLL - 1, UNROLL), step, 0)

    copies = []
    for n in range(NZ):
        for c in range(n * DEV_BLOCKS, (n + 1) * DEV_BLOCKS):
            col_scr[c, :, :HEAD_WIDTH] = dk_scr[c].astype(bf16)
            col_scr[c, :, HEAD_WIDTH:] = dv_scr[c].astype(bf16)
        part = pl.ds(n * DEV_BLOCKS, DEV_BLOCKS)
        copies += start_copies([(col_scr.at[part], col_any.at[part])], sems, 4 + n)
    for t, row_ref in enumerate((row0, row1, row2, row3)):
        for r in range(DEV_BLOCKS):
            at = lax.rem(y + t, NY) * DEV_BLOCKS + r
            cols = slice(r * BLOCK, (r + 1) * BLOCK)
            for h in range(GROUP):
                heads = slice(h * BLOCK, (h + 1) * BLOCK)
                rows = slice(h * HEAD_WIDTH, (h + 1) * HEAD_WIDTH)
                drows = slice(PAIR + h * HEAD_WIDTH, PAIR + (h + 1) * HEAD_WIDTH)
                row_scr[t, rows, cols] = o_scr[at, :, heads].astype(bf16)
                row_scr[t, drows, cols] = dq_scr[at, :, heads].astype(bf16)
        copies += start_copies([(row_scr.at[t], row_ref)], sems, 4 + NZ + t)
    for copy in copies:
        copy.wait()


def scatter_rows(part_ref, cols, value):
    y = lax.axis_index("y")
    step = value.shape[0] // (NZ * NY)
    value = value.astype(bf16)
    for i in range(NZ * NY):
        n, t = divmod(i, NY)
        part_ref[lax.rem(t - y + NY, NY), n * step : (n + 1) * step, cols] = value[i * step : (i + 1) * step]


def model_rows(i, nx, nc, width):
    head = lax.rem(lax.axis_index("x") + i % nx, nx) * nc + lax.rem(lax.axis_index("c") + i // nx, nc)
    return pl.ds(pl.multiple_of(head * width, width), width)


def rows_kernel(
    nx, nc, row0, row1, row2, row3, input_any, grad_any, wq_any, part_any, back_any, turned_any,
    got, input_ref, grad_ref, wq_ref, part_ref, back_ref, turned_ref, sems,
):
    pairs = [(row, got.at[t]) for t, row in enumerate((row0, row1, row2, row3))]
    pairs += [(input_any, input_ref), (grad_any, grad_ref), (wq_any, wq_ref)]
    copies = start_copies(pairs, sems)
    for copy in copies:
        copy.wait()
    turned_ref[...] = input_ref[...].T
    copies = start_copies([(turned_ref, turned_any)], sems, 7)
    o = sum(got[t, :PAIR, :].astype(f32) for t in range(NY)).astype(bf16)
    dq = sum(got[t, PAIR:, :].astype(f32) for t in range(NY)).astype(bf16)
    scatter_rows(part_ref, slice(0, PAIR), dot_nt(turned_ref[...], dq))
    scatter_rows(part_ref, slice(PAIR, 2 * PAIR), dot_nt(grad_ref[...].T, o))
    copies += start_copies([(part_ref, part_any)], sems, 8)
    width = wq_ref.shape[0] // (nx * nc)
    for i in range(nx * nc):
        back_ref[i * width : (i + 1) * width, :] = dot_nn(wq_ref[model_rows(i, nx, nc, width), :], dq)
    copies += start_copies([(back_ref, back_any)], sems, 9)
    for copy in copies:
        copy.wait()


def cols_kernel(got_any, turned_any, part_ref, d_ref, got_ref, turned_ref, sems):
    copies = start_copies(((got_any, got_ref), (turned_any, turned_ref)), sems)
    copies[0].wait()
    d_ref[...] = sum(got_ref[t].astype(f32) for t in range(NZ)).astype(bf16)
    copies[1].wait()
    scatter_rows(part_ref, slice(0, 2 * HEAD_WIDTH), dot_nn(turned_ref[...], d_ref[...]))


def back_kernel(nx, nc, d_ref, wk_any, wv_any, back_any, send_ref, keep_ref, wk_ref, wv_ref, back_ref, sems):
    copy_all(((wk_any, wk_ref), (wv_any, wv_ref), (back_any, back_ref)), sems)
    d = d_ref[...]
    width = wk_ref.shape[0] // (nx * nc)
    for i in range(nx * nc):
        rows = model_rows(i, nx, nc, width)
        w = jnp.concatenate([wk_ref[rows, :], wv_ref[rows, :]], axis=1)
        part = back_ref[i * width : (i + 1) * width, :] + dot_nt(w, d)
        if i < nx:
            keep_ref[i * width : (i + 1) * width, :] = part
        else:
            send_ref[(i - nx) * width : (i - nx + 1) * width, :] = part.astype(bf16)


SMEM_SPEC = pl.BlockSpec(memory_space=pltpu.SMEM)
VMEM_SPEC = pl.BlockSpec(memory_space=pltpu.VMEM)
HBM_SPEC = pl.BlockSpec(memory_space=pltpu.HBM)


def vmem(mib):
    return pltpu.CompilerParams(vmem_limit_bytes=mib * 1024 * 1024)


STACK = jax.ShapeDtypeStruct((ROW_BLOCKS, PAIR, 2 * HEAD_WIDTH), bf16)


def join_call(keys, values):
    return pl.pallas_call(
        join_kernel,
        out_shape=jax.ShapeDtypeStruct((keys.shape[0], 2 * HEAD_WIDTH), bf16),
        in_specs=[HBM_SPEC] * 2,
        out_specs=VMEM_SPEC,
        scratch_shapes=[pltpu.SemaphoreType.DMA((2,))],
        compiler_params=vmem(54),
        name="join",
    )(keys, values)


def start_call(queries, grad_out, output_weight):
    return pl.pallas_call(
        start_kernel,
        out_shape=jax.ShapeDtypeStruct((queries.shape[0], 2 * PAIR), bf16),
        in_specs=[HBM_SPEC] * 3,
        out_specs=VMEM_SPEC,
        scratch_shapes=[
            pltpu.VMEM(grad_out.shape, bf16),
            pltpu.VMEM(output_weight.shape, bf16),
            pltpu.SemaphoreType.DMA((3,)),
        ],
        compiler_params=vmem(54),
        name="start",
    )(queries, grad_out, output_weight)


def plan_call(anc):
    return pl.pallas_call(
        plan_kernel,
        out_shape=jax.ShapeDtypeStruct((PLAN,), jnp.int32),
        in_specs=[SMEM_SPEC],
        out_specs=SMEM_SPEC,
        name="plan",
    )(anc)


def stack_call(qds):
    return pl.pallas_call(
        stack_kernel,
        out_shape=STACK,
        in_specs=[HBM_SPEC] * 5,
        out_specs=HBM_SPEC,
        scratch_shapes=[pltpu.SemaphoreType.DMA((2 * GROUP * (3 * DEV_BLOCKS + 4),))],
        compiler_params=vmem(4),
        name="stack",
    )(*qds)


def stats_call(plan, pieces, qd):
    return pl.pallas_call(
        stats_kernel,
        out_shape=(
            jax.ShapeDtypeStruct((3 * STAT_ROWS, PAIR), f32),
            jax.ShapeDtypeStruct((COL_BLOCKS, BLOCK, 2 * HEAD_WIDTH), bf16),
        ),
        in_specs=[HBM_SPEC] * 10 + [VMEM_SPEC],
        out_specs=(VMEM_SPEC, VMEM_SPEC),
        scratch_shapes=[
            pltpu.SMEM((PLAN,), jnp.int32),
            pltpu.SemaphoreType.DMA((12,)),
        ],
        compiler_params=vmem(12),
        name="stats",
    )(plan, *pieces, qd)


def grads_call(plan, kv, qd, stats):
    return pl.pallas_call(
        grads_kernel,
        out_shape=(
            *[jax.ShapeDtypeStruct((2 * PAIR, DEV_BLOCKS * BLOCK), bf16)] * NY,
            jax.ShapeDtypeStruct((COL_BLOCKS, BLOCK, 2 * HEAD_WIDTH), bf16),
        ),
        in_specs=[HBM_SPEC] * 3 + [VMEM_SPEC] * 4,
        out_specs=(HBM_SPEC,) * 5,
        scratch_shapes=[
            pltpu.VMEM((ROW_BLOCKS, HEAD_WIDTH, PAIR), f32),
            pltpu.VMEM((ROW_BLOCKS, HEAD_WIDTH, PAIR), f32),
            pltpu.VMEM((COL_BLOCKS, BLOCK, HEAD_WIDTH), f32),
            pltpu.VMEM((COL_BLOCKS, BLOCK, HEAD_WIDTH), f32),
            pltpu.VMEM((STAT_ROWS, PAIR), f32),
            pltpu.VMEM((STAT_ROWS, PAIR), f32),
            pltpu.VMEM((COL_BLOCKS, BLOCK, 2 * HEAD_WIDTH), bf16),
            pltpu.VMEM((COL_BLOCKS, 2 * HEAD_WIDTH, BLOCK), bf16),
            pltpu.VMEM(STACK.shape, bf16),
            pltpu.SMEM((PLAN,), jnp.int32),
            pltpu.VMEM((NY, 2 * PAIR, DEV_BLOCKS * BLOCK), bf16),
            pltpu.VMEM((COL_BLOCKS, BLOCK, 2 * HEAD_WIDTH), bf16),
            pltpu.SemaphoreType.DMA((4 + NZ + NY,)),
        ],
        compiler_params=vmem(40),
        name="grads",
    )(plan, kv, qd, *stats)


def shift(x, axis, size, by):
    return lax.ppermute(x, axis, [(i, (i + by) % size) for i in range(size)])


def rows_call(nx, nc, got, normed_input, grad_out, query_weight):
    tokens, model = normed_input.shape
    return pl.pallas_call(
        functools.partial(rows_kernel, nx, nc),
        out_shape=(
            jax.ShapeDtypeStruct((NY, model // NY, 2 * PAIR), bf16),
            jax.ShapeDtypeStruct((model, tokens), f32),
            jax.ShapeDtypeStruct((model, tokens), bf16),
        ),
        in_specs=[HBM_SPEC] * 7,
        out_specs=(HBM_SPEC,) * 3,
        scratch_shapes=[
            pltpu.VMEM((NY, 2 * PAIR, tokens), bf16),
            pltpu.VMEM(normed_input.shape, bf16),
            pltpu.VMEM(normed_input.shape, bf16),
            pltpu.VMEM(query_weight.shape, bf16),
            pltpu.VMEM((NY, model // NY, 2 * PAIR), bf16),
            pltpu.VMEM((model, tokens), f32),
            pltpu.VMEM((model, tokens), bf16),
            pltpu.SemaphoreType.DMA((10,)),
        ],
        compiler_params=vmem(54),
        name="rows",
    )(*got, normed_input, grad_out, query_weight)


def cols_call(got, turned):
    model, tokens = turned.shape
    return pl.pallas_call(
        cols_kernel,
        out_shape=(
            jax.ShapeDtypeStruct((NY, model // NY, 2 * HEAD_WIDTH), bf16),
            jax.ShapeDtypeStruct((tokens, 2 * HEAD_WIDTH), bf16),
        ),
        in_specs=[HBM_SPEC] * 2,
        out_specs=(VMEM_SPEC,) * 2,
        scratch_shapes=[
            pltpu.VMEM(got.shape, bf16),
            pltpu.VMEM(turned.shape, bf16),
            pltpu.SemaphoreType.DMA((2,)),
        ],
        compiler_params=vmem(20),
        name="cols",
    )(got, turned)


def back_call(nx, nc, d, key_weight, value_weight, back):
    model, tokens = back.shape
    side = model // nc
    return pl.pallas_call(
        functools.partial(back_kernel, nx, nc),
        out_shape=(
            jax.ShapeDtypeStruct((max(model - side, side), tokens), bf16),
            jax.ShapeDtypeStruct((side, tokens), f32),
        ),
        in_specs=[VMEM_SPEC] + [HBM_SPEC] * 3,
        out_specs=(VMEM_SPEC,) * 2,
        scratch_shapes=[
            pltpu.VMEM(key_weight.shape, bf16),
            pltpu.VMEM(value_weight.shape, bf16),
            pltpu.VMEM(back.shape, f32),
            pltpu.SemaphoreType.DMA((3,)),
        ],
        compiler_params=vmem(20),
        name="back",
    )(d, key_weight, value_weight, back)


def ring_gather(own):
    up, down = [own], [own]
    for _ in range(3):
        up.append(shift(up[-1], "z", NZ, 1))
        down.append(shift(down[-1], "z", NZ, -1))
    pieces = [p.reshape(DEV_BLOCKS, BLOCK, 2 * HEAD_WIDTH) for p in up + down[:0:-1]]
    top = shift(up[-1][: 2 * BLOCK], "z", NZ, 1)
    bottom = shift(down[-1][BLOCK:], "z", NZ, -1)
    return pieces + [top.reshape(2, BLOCK, 2 * HEAD_WIDTH), bottom.reshape(2, BLOCK, 2 * HEAD_WIDTH)]


def per_device(
    nx, nc, normed_input, queries, keys, values, grad_out, query_weight, key_weight, value_weight, output_weight, ancestors
):
    model = grad_out.shape[1]

    pieces = ring_gather(join_call(keys, values))
    mine = start_call(queries, grad_out, output_weight)
    before, after = shift(mine, "y", NY, 1), shift(mine, "y", NY, -1)
    half = mine.shape[0] // 2
    qds = [mine, before, after, shift(before[:half], "y", NY, 1), shift(after[half:], "y", NY, -1)]

    plan = plan_call(ancestors.T)
    qd = stack_call(qds)
    own, kv = stats_call(plan, pieces, qd)
    stats = [own] + [shift(own, "y", NY, s) for s in range(1, NY)]
    *row_part, col_part = grads_call(plan, kv, qd, stats)

    col_got = lax.all_to_all(col_part.reshape(NZ, DEV_BLOCKS * BLOCK, 2 * HEAD_WIDTH), "z", 0, 0, tiled=True)
    row_got = [row_part[0]] + [shift(row_part[s], "y", NY, s) for s in range(1, NY)]

    part_rows = model // (NZ * NY)
    qo_part, back, turned = rows_call(nx, nc, row_got, normed_input, grad_out, query_weight)
    qo_got = [qo_part[0]] + [shift(qo_part[s], "y", NY, s) for s in range(1, NY)]

    kv_part, dkv = cols_call(col_got, turned)
    send, keep = back_call(nx, nc, dkv, key_weight, value_weight, back)
    kv_got = [kv_part[0]] + [shift(kv_part[s], "y", NY, s) for s in range(1, NY)]
    sums = [sum(g.astype(f32) for g in got).astype(bf16) for got in (qo_got, kv_got)]
    sums = jnp.concatenate(sums, axis=1).reshape(NZ, part_rows, 2 * PAIR + 2 * HEAD_WIDTH)
    sums = jnp.sum(lax.all_to_all(sums, "z", 0, 0, tiled=True).astype(f32), axis=0)

    width = model // (nx * nc)
    side = nx * width
    for s in range(1, nc):
        keep = keep + shift(send[(s - 1) * side : s * side], "c", nc, s).astype(f32)
    input_grad = keep[:width]
    for s in range(1, nx):
        piece = keep[s * width : (s + 1) * width].astype(bf16)
        input_grad = input_grad + shift(piece, "x", nx, s).astype(f32)
    return (
        input_grad.astype(bf16).T,
        sums[:, :PAIR],
        sums[:, 2 * PAIR : 2 * PAIR + HEAD_WIDTH],
        sums[:, 2 * PAIR + HEAD_WIDTH :],
        sums[:, PAIR : 2 * PAIR].T,
    )


def solution(mesh):
    heads = mesh.shape["head"]
    nc = 2 if heads % 2 == 0 else 1
    nx = heads // nc
    grid = Mesh(mesh.devices.reshape(NZ, NY, nx, nc), ("z", "y", "x", "c"))
    leaf, head = ("z", "y"), ("x", "c")
    return jax.shard_map(
        functools.partial(per_device, nx, nc),
        mesh=grid,
        in_specs=(
            P(leaf, None),
            P(leaf, head),
            P(leaf, head),
            P(leaf, head),
            P(leaf, None),
            P(None, head),
            P(None, head),
            P(None, head),
            P(head, None),
            P(),
        ),
        out_specs=(
            P(leaf, head),
            P(leaf, head),
            P(leaf, head),
            P(leaf, head),
            P(head, leaf),
        ),
        check_vma=False,
    )
```

```python
import functools
import math

import jax
import jax.numpy as jnp
from jax import lax
from jax.experimental import pallas as pl
from jax.experimental.pallas import tpu as pltpu
from jax.sharding import Mesh, PartitionSpec as P

HEAD_WIDTH = 128
BLOCK = 128
GROUP = 2
NZ, NY = 8, 4
DEV_BLOCKS = 3
ROW_BLOCKS = NY * DEV_BLOCKS
COL_BLOCKS = NZ * DEV_BLOCKS
PATH = 16
PAIR = GROUP * BLOCK
SCALE = HEAD_WIDTH ** (-0.5)
SCALE2 = SCALE * math.log2(math.e)
NEG = -1e30
STAT_ROWS = 16
SLOTS = 2
UNROLL = 4
ENTRIES = 256
AT, SLOT, REACH, COUNT = 0, ENTRIES, 2 * ENTRIES, 3 * ENTRIES
PLAN = COUNT + 128

f32 = jnp.float32
bf16 = jnp.bfloat16


def dot_nt(a, b):
    return lax.dot_general(a, b, (((1,), (1,)), ((), ())), preferred_element_type=f32)


def dot_nn(a, b):
    return jnp.dot(a, b, preferred_element_type=f32)


def start_copies(pairs, sems, first=0):
    copies = [pltpu.make_async_copy(src, dst, sems.at[first + i]) for i, (src, dst) in enumerate(pairs)]
    for copy in copies:
        copy.start()
    return copies


def copy_all(pairs, sems):
    for copy in start_copies(pairs, sems):
        copy.wait()


def join_kernel(key_any, value_any, kv_ref, sems):
    copy_all(
        (
            (key_any, kv_ref.at[:, pl.ds(0, HEAD_WIDTH)]),
            (value_any, kv_ref.at[:, pl.ds(HEAD_WIDTH, HEAD_WIDTH)]),
        ),
        sems,
    )


def start_kernel(query_any, grad_any, weight_any, qd_ref, grad_ref, weight_ref, sems):
    pairs = ((grad_any, grad_ref), (weight_any, weight_ref), (query_any, qd_ref.at[:, pl.ds(0, PAIR)]))
    copies = start_copies(pairs, sems)
    copies[0].wait()
    copies[1].wait()
    qd_ref[:, PAIR:] = dot_nt(grad_ref[...], weight_ref[...]).astype(bf16)
    copies[2].wait()


def stack_kernel(own, before, after, top, bottom, out_ref, sems):
    y = lax.axis_index("y")
    pairs = []

    def put(src, src_row, back, row, count):
        at = lax.rem(y - back + NY, NY) * DEV_BLOCKS + row // BLOCK
        for k in range(2):
            for h in range(GROUP):
                src_cols = pl.ds(k * PAIR + h * HEAD_WIDTH, HEAD_WIDTH)
                dst = out_ref.at[at, pl.ds(h * BLOCK + row % BLOCK, count), pl.ds(k * HEAD_WIDTH, HEAD_WIDTH)]
                pairs.append((src.at[pl.ds(src_row, count), src_cols], dst))

    half = BLOCK // 2
    for src, back in ((own, 0), (before, 1), (after, 3)):
        for r in range(DEV_BLOCKS):
            put(src, r * BLOCK, back, r * BLOCK, BLOCK)
    put(top, 0, 2, 0, BLOCK)
    put(top, BLOCK, 2, BLOCK, half)
    put(bottom, 0, 2, BLOCK + half, half)
    put(bottom, half, 2, 2 * BLOCK, BLOCK)
    copy_all(pairs, sems)


def plan_kernel(anc_ref, plan_ref):
    z, y = lax.axis_index("z"), lax.axis_index("y")

    def put(e, at, slot, reach):
        plan_ref[AT + e] = at
        plan_ref[SLOT + e] = slot
        plan_ref[REACH + e] = reach

    def one_block(at, first):
        block = z * ROW_BLOCKS + at

        def one_key(j, e):
            c = anc_ref[j, block]
            device = lax.div(c, DEV_BLOCKS)
            row = lax.div(device, NY)
            hit = jnp.logical_and(c >= 0, device - row * NY == y)
            slot = row * DEV_BLOCKS + c - device * DEV_BLOCKS
            put(e, at, slot, jnp.where(c == block, 0, BLOCK))
            return e + hit.astype(jnp.int32)

        e = lax.fori_loop(0, PATH, one_key, first, unroll=True)
        put(e, at, 0, -BLOCK)
        return e + lax.rem(e, SLOTS)

    end = lax.fori_loop(0, ROW_BLOCKS, one_block, jnp.int32(0))
    for u in range(SLOTS * UNROLL):
        put(end + u, 0, 0, -BLOCK)
    plan_ref[COUNT] = lax.div(end, SLOTS)


def group_of(plan_ref, g):
    slots = [plan_ref[SLOT + SLOTS * g + k] for k in range(SLOTS)]
    reach = [plan_ref[REACH + SLOTS * g + k] for k in range(SLOTS)]
    return plan_ref[AT + SLOTS * g], slots, reach


def base2_scores(kv_ref, q, slots, reach):
    keys = jnp.concatenate([kv_ref[s, :, :HEAD_WIDTH] for s in slots], axis=0)
    s = dot_nt(keys, q) * SCALE2
    key_at = lax.broadcasted_iota(jnp.int32, (BLOCK, PAIR), 0)
    query_at = lax.rem(lax.broadcasted_iota(jnp.int32, (BLOCK, PAIR), 1), BLOCK)
    behind = key_at - query_at
    hide = jnp.concatenate([behind > r for r in reach], axis=0)
    return jnp.where(hide, NEG, s)


def value_dot(kv_ref, d, slots):
    return dot_nt(jnp.concatenate([kv_ref[s, :, HEAD_WIDTH:] for s in slots], axis=0), d)


def stats_kernel(plan_any, *refs):
    pieces, (qd_ref, out_ref, kv_ref, plan_ref, sems) = refs[:9], refs[9:]
    z = lax.axis_index("z")

    def slots_of(back):
        return pl.ds(lax.rem(z - back + NZ, NZ) * DEV_BLOCKS, DEV_BLOCKS)

    pairs = [(plan_any, plan_ref)]
    for piece, back in zip(pieces[:7], (0, 1, 2, 3, 5, 6, 7)):
        pairs.append((piece, kv_ref.at[slots_of(back)]))
    far = lax.rem(z + NZ // 2, NZ) * DEV_BLOCKS
    half = BLOCK // 2
    pairs.append((pieces[7].at[0:1], kv_ref.at[pl.ds(far, 1)]))
    pairs.append((pieces[7].at[1, pl.ds(0, half)], kv_ref.at[far + 1, pl.ds(0, half)]))
    pairs.append((pieces[8].at[0, pl.ds(half, half)], kv_ref.at[far + 1, pl.ds(half, half)]))
    pairs.append((pieces[8].at[1:2], kv_ref.at[pl.ds(far + 2, 1)]))
    copy_all(pairs, sems)
    out_ref[0:STAT_ROWS, :] = jnp.full((STAT_ROWS, PAIR), NEG, f32)
    out_ref[STAT_ROWS:, :] = jnp.zeros((2 * STAT_ROWS, PAIR), f32)

    def step(i, _):
        done = []
        for u in range(UNROLL):
            at, slots, reach = group_of(plan_ref, i * UNROLL + u)
            s = base2_scores(kv_ref, qd_ref[at, :, :HEAD_WIDTH], slots, reach)
            g = value_dot(kv_ref, qd_ref[at, :, HEAD_WIDTH:], slots)
            m = jnp.max(s, axis=0, keepdims=True)
            p = jnp.exp2(s - m)
            done.append((at, m, jnp.sum(p, axis=0, keepdims=True), jnp.sum(p * g, axis=0, keepdims=True)))
        for at, m, total, dsum in done:
            rows = [pl.ds(n * STAT_ROWS + at, 1) for n in range(3)]
            before = out_ref[rows[0], :]
            top = jnp.maximum(before, m)
            old, new = jnp.exp2(before - top), jnp.exp2(m - top)
            out_ref[rows[0], :] = top
            out_ref[rows[1], :] = out_ref[rows[1], :] * old + total * new
            out_ref[rows[2], :] = out_ref[rows[2], :] * old + dsum * new
        return 0

    lax.fori_loop(0, lax.div(plan_ref[COUNT] + UNROLL - 1, UNROLL), step, 0)


def grads_kernel(
    plan_any, kv_any, qd_any, st0, st1, st2, st3,
    row0, row1, row2, row3, col_any,
    o_scr, dq_scr, dk_scr, dv_scr, lse_scr, delta_scr,
    kv_ref, kvt_ref, qd_ref, plan_ref, row_scr, col_scr, sems,
):
    y = lax.axis_index("y")
    pairs = ((kv_any, kv_ref), (qd_any, qd_ref), (plan_any, plan_ref))
    copies = start_copies(pairs, sems)
    for scr in (o_scr, dq_scr, dk_scr, dv_scr):
        def clear(i, _, scr=scr):
            scr[i] = jnp.zeros(scr.shape[1:], f32)
            return 0

        lax.fori_loop(0, scr.shape[0], clear, 0)

    tops = [st[0:STAT_ROWS, :] for st in (st0, st1, st2, st3)]
    m = functools.reduce(jnp.maximum, tops)
    factors = [jnp.exp2(t - m) for t in tops]
    total, dsum = (
        sum(st[n * STAT_ROWS : (n + 1) * STAT_ROWS, :] * f for st, f in zip((st0, st1, st2, st3), factors))
        for n in (1, 2)
    )
    lse_scr[...] = m + jnp.log2(total)
    delta_scr[...] = dsum / total
    copies[0].wait()

    def turn(c, _):
        for k in range(2):
            cols = slice(k * HEAD_WIDTH, (k + 1) * HEAD_WIDTH)
            kvt_ref[c, cols, :] = kv_ref[c, :, cols].T
        return 0

    lax.fori_loop(0, COL_BLOCKS, turn, 0, unroll=4)
    for copy in copies[1:]:
        copy.wait()

    def step(i, _):
        done = []
        for u in range(UNROLL):
            at, slots, reach = group_of(plan_ref, i * UNROLL + u)
            q, d = qd_ref[at, :, :HEAD_WIDTH], qd_ref[at, :, HEAD_WIDTH:]
            w = jnp.exp2(base2_scores(kv_ref, q, slots, reach) - lse_scr[pl.ds(at, 1), :])
            g = value_dot(kv_ref, d, slots)
            p = w.astype(bf16)
            ds = (w * (g - delta_scr[pl.ds(at, 1), :]) * SCALE).astype(bf16)
            kt = jnp.concatenate([kvt_ref[s, :HEAD_WIDTH, :] for s in slots], axis=1)
            vt = jnp.concatenate([kvt_ref[s, HEAD_WIDTH:, :] for s in slots], axis=1)
            done.append((at, slots, dot_nn(vt, p), dot_nn(kt, ds), dot_nn(ds, q), dot_nn(p, d)))
        for at, slots, o, dq, dk, dv in done:
            o_scr[at] += o
            dq_scr[at] += dq
            for k, slot in enumerate(slots):
                dk_scr[slot] += dk[k * BLOCK : (k + 1) * BLOCK]
                dv_scr[slot] += dv[k * BLOCK : (k + 1) * BLOCK]
        return 0

    lax.fori_loop(0, lax.div(plan_ref[COUNT] + UNROLL - 1, UNROLL), step, 0)

    copies = []
    for n in range(NZ):
        for c in range(n * DEV_BLOCKS, (n + 1) * DEV_BLOCKS):
            col_scr[c, :, :HEAD_WIDTH] = dk_scr[c].astype(bf16)
            col_scr[c, :, HEAD_WIDTH:] = dv_scr[c].astype(bf16)
        part = pl.ds(n * DEV_BLOCKS, DEV_BLOCKS)
        copies += start_copies([(col_scr.at[part], col_any.at[part])], sems, 4 + n)
    for t, row_ref in enumerate((row0, row1, row2, row3)):
        for r in range(DEV_BLOCKS):
            at = lax.rem(y + t, NY) * DEV_BLOCKS + r
            cols = slice(r * BLOCK, (r + 1) * BLOCK)
            for h in range(GROUP):
                heads = slice(h * BLOCK, (h + 1) * BLOCK)
                rows = slice(h * HEAD_WIDTH, (h + 1) * HEAD_WIDTH)
                drows = slice(PAIR + h * HEAD_WIDTH, PAIR + (h + 1) * HEAD_WIDTH)
                row_scr[t, rows, cols] = o_scr[at, :, heads].astype(bf16)
                row_scr[t, drows, cols] = dq_scr[at, :, heads].astype(bf16)
        copies += start_copies([(row_scr.at[t], row_ref)], sems, 4 + NZ + t)
    for copy in copies:
        copy.wait()


def scatter_rows(part_ref, cols, value):
    y = lax.axis_index("y")
    step = value.shape[0] // (NZ * NY)
    value = value.astype(bf16)
    for i in range(NZ * NY):
        n, t = divmod(i, NY)
        part_ref[lax.rem(t - y + NY, NY), n * step : (n + 1) * step, cols] = value[i * step : (i + 1) * step]


def model_rows(i, nx, nc, width):
    head = lax.rem(lax.axis_index("x") + i % nx, nx) * nc + lax.rem(lax.axis_index("c") + i // nx, nc)
    return pl.ds(pl.multiple_of(head * width, width), width)


def rows_kernel(
    nx, nc, row0, row1, row2, row3, input_any, grad_any, wq_any, part_any, back_any, turned_any,
    got, input_ref, grad_ref, wq_ref, part_ref, back_ref, turned_ref, sems,
):
    pairs = [(row, got.at[t]) for t, row in enumerate((row0, row1, row2, row3))]
    pairs += [(input_any, input_ref), (grad_any, grad_ref), (wq_any, wq_ref)]
    copies = start_copies(pairs, sems)
    for copy in copies:
        copy.wait()
    turned_ref[...] = input_ref[...].T
    copies = start_copies([(turned_ref, turned_any)], sems, 7)
    o = sum(got[t, :PAIR, :].astype(f32) for t in range(NY)).astype(bf16)
    dq = sum(got[t, PAIR:, :].astype(f32) for t in range(NY)).astype(bf16)
    scatter_rows(part_ref, slice(0, PAIR), dot_nt(turned_ref[...], dq))
    scatter_rows(part_ref, slice(PAIR, 2 * PAIR), dot_nt(grad_ref[...].T, o))
    copies += start_copies([(part_ref, part_any)], sems, 8)
    width = wq_ref.shape[0] // (nx * nc)
    for i in range(nx * nc):
        back_ref[i * width : (i + 1) * width, :] = dot_nn(wq_ref[model_rows(i, nx, nc, width), :], dq)
    copies += start_copies([(back_ref, back_any)], sems, 9)
    for copy in copies:
        copy.wait()


def cols_kernel(got_any, turned_any, part_ref, d_ref, got_ref, turned_ref, sems):
    copies = start_copies(((got_any, got_ref), (turned_any, turned_ref)), sems)
    copies[0].wait()
    d_ref[...] = sum(got_ref[t].astype(f32) for t in range(NZ)).astype(bf16)
    copies[1].wait()
    scatter_rows(part_ref, slice(0, 2 * HEAD_WIDTH), dot_nn(turned_ref[...], d_ref[...]))


def back_kernel(nx, nc, d_ref, wk_any, wv_any, back_any, send_ref, keep_ref, wk_ref, wv_ref, back_ref, sems):
    copy_all(((wk_any, wk_ref), (wv_any, wv_ref), (back_any, back_ref)), sems)
    d = d_ref[...]
    width = wk_ref.shape[0] // (nx * nc)
    for i in range(nx * nc):
        rows = model_rows(i, nx, nc, width)
        w = jnp.concatenate([wk_ref[rows, :], wv_ref[rows, :]], axis=1)
        part = back_ref[i * width : (i + 1) * width, :] + dot_nt(w, d)
        if i < nx:
            keep_ref[i * width : (i + 1) * width, :] = part
        else:
            send_ref[(i - nx) * width : (i - nx + 1) * width, :] = part.astype(bf16)


SMEM_SPEC = pl.BlockSpec(memory_space=pltpu.SMEM)
VMEM_SPEC = pl.BlockSpec(memory_space=pltpu.VMEM)
HBM_SPEC = pl.BlockSpec(memory_space=pltpu.HBM)


def vmem(mib):
    return pltpu.CompilerParams(vmem_limit_bytes=mib * 1024 * 1024)


STACK = jax.ShapeDtypeStruct((ROW_BLOCKS, PAIR, 2 * HEAD_WIDTH), bf16)


def join_call(keys, values):
    return pl.pallas_call(
        join_kernel,
        out_shape=jax.ShapeDtypeStruct((keys.shape[0], 2 * HEAD_WIDTH), bf16),
        in_specs=[HBM_SPEC] * 2,
        out_specs=VMEM_SPEC,
        scratch_shapes=[pltpu.SemaphoreType.DMA((2,))],
        compiler_params=vmem(54),
        name="join",
    )(keys, values)


def start_call(queries, grad_out, output_weight):
    return pl.pallas_call(
        start_kernel,
        out_shape=jax.ShapeDtypeStruct((queries.shape[0], 2 * PAIR), bf16),
        in_specs=[HBM_SPEC] * 3,
        out_specs=VMEM_SPEC,
        scratch_shapes=[
            pltpu.VMEM(grad_out.shape, bf16),
            pltpu.VMEM(output_weight.shape, bf16),
            pltpu.SemaphoreType.DMA((3,)),
        ],
        compiler_params=vmem(54),
        name="start",
    )(queries, grad_out, output_weight)


def plan_call(anc):
    return pl.pallas_call(
        plan_kernel,
        out_shape=jax.ShapeDtypeStruct((PLAN,), jnp.int32),
        in_specs=[SMEM_SPEC],
        out_specs=SMEM_SPEC,
        name="plan",
    )(anc)


def stack_call(qds):
    return pl.pallas_call(
        stack_kernel,
        out_shape=STACK,
        in_specs=[HBM_SPEC] * 5,
        out_specs=HBM_SPEC,
        scratch_shapes=[pltpu.SemaphoreType.DMA((2 * GROUP * (3 * DEV_BLOCKS + 4),))],
        compiler_params=vmem(4),
        name="stack",
    )(*qds)


def stats_call(plan, pieces, qd):
    return pl.pallas_call(
        stats_kernel,
        out_shape=(
            jax.ShapeDtypeStruct((3 * STAT_ROWS, PAIR), f32),
            jax.ShapeDtypeStruct((COL_BLOCKS, BLOCK, 2 * HEAD_WIDTH), bf16),
        ),
        in_specs=[HBM_SPEC] * 10 + [VMEM_SPEC],
        out_specs=(VMEM_SPEC, VMEM_SPEC),
        scratch_shapes=[
            pltpu.SMEM((PLAN,), jnp.int32),
            pltpu.SemaphoreType.DMA((12,)),
        ],
        compiler_params=vmem(12),
        name="stats",
    )(plan, *pieces, qd)


def grads_call(plan, kv, qd, stats):
    return pl.pallas_call(
        grads_kernel,
        out_shape=(
            *[jax.ShapeDtypeStruct((2 * PAIR, DEV_BLOCKS * BLOCK), bf16)] * NY,
            jax.ShapeDtypeStruct((COL_BLOCKS, BLOCK, 2 * HEAD_WIDTH), bf16),
        ),
        in_specs=[HBM_SPEC] * 3 + [VMEM_SPEC] * 4,
        out_specs=(HBM_SPEC,) * 5,
        scratch_shapes=[
            pltpu.VMEM((ROW_BLOCKS, HEAD_WIDTH, PAIR), f32),
            pltpu.VMEM((ROW_BLOCKS, HEAD_WIDTH, PAIR), f32),
            pltpu.VMEM((COL_BLOCKS, BLOCK, HEAD_WIDTH), f32),
            pltpu.VMEM((COL_BLOCKS, BLOCK, HEAD_WIDTH), f32),
            pltpu.VMEM((STAT_ROWS, PAIR), f32),
            pltpu.VMEM((STAT_ROWS, PAIR), f32),
            pltpu.VMEM((COL_BLOCKS, BLOCK, 2 * HEAD_WIDTH), bf16),
            pltpu.VMEM((COL_BLOCKS, 2 * HEAD_WIDTH, BLOCK), bf16),
            pltpu.VMEM(STACK.shape, bf16),
            pltpu.SMEM((PLAN,), jnp.int32),
            pltpu.VMEM((NY, 2 * PAIR, DEV_BLOCKS * BLOCK), bf16),
            pltpu.VMEM((COL_BLOCKS, BLOCK, 2 * HEAD_WIDTH), bf16),
            pltpu.SemaphoreType.DMA((4 + NZ + NY,)),
        ],
        compiler_params=vmem(40),
        name="grads",
    )(plan, kv, qd, *stats)


def shift(x, axis, size, by):
    return lax.ppermute(x, axis, [(i, (i + by) % size) for i in range(size)])


def rows_call(nx, nc, got, normed_input, grad_out, query_weight):
    tokens, model = normed_input.shape
    return pl.pallas_call(
        functools.partial(rows_kernel, nx, nc),
        out_shape=(
            jax.ShapeDtypeStruct((NY, model // NY, 2 * PAIR), bf16),
            jax.ShapeDtypeStruct((model, tokens), f32),
            jax.ShapeDtypeStruct((model, tokens), bf16),
        ),
        in_specs=[HBM_SPEC] * 7,
        out_specs=(HBM_SPEC,) * 3,
        scratch_shapes=[
            pltpu.VMEM((NY, 2 * PAIR, tokens), bf16),
            pltpu.VMEM(normed_input.shape, bf16),
            pltpu.VMEM(normed_input.shape, bf16),
            pltpu.VMEM(query_weight.shape, bf16),
            pltpu.VMEM((NY, model // NY, 2 * PAIR), bf16),
            pltpu.VMEM((model, tokens), f32),
            pltpu.VMEM((model, tokens), bf16),
            pltpu.SemaphoreType.DMA((10,)),
        ],
        compiler_params=vmem(54),
        name="rows",
    )(*got, normed_input, grad_out, query_weight)


def cols_call(got, turned):
    model, tokens = turned.shape
    return pl.pallas_call(
        cols_kernel,
        out_shape=(
            jax.ShapeDtypeStruct((NY, model // NY, 2 * HEAD_WIDTH), bf16),
            jax.ShapeDtypeStruct((tokens, 2 * HEAD_WIDTH), bf16),
        ),
        in_specs=[HBM_SPEC] * 2,
        out_specs=(VMEM_SPEC,) * 2,
        scratch_shapes=[
            pltpu.VMEM(got.shape, bf16),
            pltpu.VMEM(turned.shape, bf16),
            pltpu.SemaphoreType.DMA((2,)),
        ],
        compiler_params=vmem(20),
        name="cols",
    )(got, turned)


def back_call(nx, nc, d, key_weight, value_weight, back):
    model, tokens = back.shape
    side = model // nc
    return pl.pallas_call(
        functools.partial(back_kernel, nx, nc),
        out_shape=(
            jax.ShapeDtypeStruct((max(model - side, side), tokens), bf16),
            jax.ShapeDtypeStruct((side, tokens), f32),
        ),
        in_specs=[VMEM_SPEC] + [HBM_SPEC] * 3,
        out_specs=(VMEM_SPEC,) * 2,
        scratch_shapes=[
            pltpu.VMEM(key_weight.shape, bf16),
            pltpu.VMEM(value_weight.shape, bf16),
            pltpu.VMEM(back.shape, f32),
            pltpu.SemaphoreType.DMA((3,)),
        ],
        compiler_params=vmem(20),
        name="back",
    )(d, key_weight, value_weight, back)


def ring_gather(own, plan):
    up, down = [own], [own]
    for step in range(3):
        up.append(shift(up[-1], "z", NZ, 1))
        down.append(shift(down[-1], "z", NZ, -1))
        if step == 1:
            up[-1], plan = lax.optimization_barrier((up[-1], plan))
    pieces = [p.reshape(DEV_BLOCKS, BLOCK, 2 * HEAD_WIDTH) for p in up + down[:0:-1]]
    top = shift(up[-1][: 2 * BLOCK], "z", NZ, 1)
    bottom = shift(down[-1][BLOCK:], "z", NZ, -1)
    return plan, pieces + [top.reshape(2, BLOCK, 2 * HEAD_WIDTH), bottom.reshape(2, BLOCK, 2 * HEAD_WIDTH)]


def per_device(
    nx, nc, normed_input, queries, keys, values, grad_out, query_weight, key_weight, value_weight, output_weight, ancestors
):
    model = grad_out.shape[1]

    plan, pieces = ring_gather(join_call(keys, values), plan_call(ancestors.T))
    mine = start_call(queries, grad_out, output_weight)
    before, after = shift(mine, "y", NY, 1), shift(mine, "y", NY, -1)
    half = mine.shape[0] // 2
    qds = [mine, before, after, shift(before[:half], "y", NY, 1), shift(after[half:], "y", NY, -1)]

    qd = stack_call(qds)
    own, kv = stats_call(plan, pieces, qd)
    stats = [own] + [shift(own, "y", NY, s) for s in range(1, NY)]
    *row_part, col_part = grads_call(plan, kv, qd, stats)

    col_got = lax.all_to_all(col_part.reshape(NZ, DEV_BLOCKS * BLOCK, 2 * HEAD_WIDTH), "z", 0, 0, tiled=True)
    row_got = [row_part[0]] + [shift(row_part[s], "y", NY, s) for s in range(1, NY)]

    part_rows = model // (NZ * NY)
    qo_part, back, turned = rows_call(nx, nc, row_got, normed_input, grad_out, query_weight)
    qo_got = [qo_part[0]] + [shift(qo_part[s], "y", NY, s) for s in range(1, NY)]

    kv_part, dkv = cols_call(col_got, turned)
    send, keep = back_call(nx, nc, dkv, key_weight, value_weight, back)
    kv_got = [kv_part[0]] + [shift(kv_part[s], "y", NY, s) for s in range(1, NY)]
    sums = [sum(g.astype(f32) for g in got).astype(bf16) for got in (qo_got, kv_got)]
    sums = jnp.concatenate(sums, axis=1).reshape(NZ, part_rows, 2 * PAIR + 2 * HEAD_WIDTH)
    sums = jnp.sum(lax.all_to_all(sums, "z", 0, 0, tiled=True).astype(f32), axis=0)

    width = model // (nx * nc)
    side = nx * width
    for s in range(1, nc):
        keep = keep + shift(send[(s - 1) * side : s * side], "c", nc, s).astype(f32)
    input_grad = keep[:width]
    for s in range(1, nx):
        piece = keep[s * width : (s + 1) * width].astype(bf16)
        input_grad = input_grad + shift(piece, "x", nx, s).astype(f32)
    return (
        input_grad.astype(bf16).T,
        sums[:, :PAIR],
        sums[:, 2 * PAIR : 2 * PAIR + HEAD_WIDTH],
        sums[:, 2 * PAIR + HEAD_WIDTH :],
        sums[:, PAIR : 2 * PAIR].T,
    )


def solution(mesh):
    heads = mesh.shape["head"]
    nc = 2 if heads % 2 == 0 else 1
    nx = heads // nc
    grid = Mesh(mesh.devices.reshape(NZ, NY, nx, nc), ("z", "y", "x", "c"))
    leaf, head = ("z", "y"), ("x", "c")
    return jax.shard_map(
        functools.partial(per_device, nx, nc),
        mesh=grid,
        in_specs=(
            P(leaf, None),
            P(leaf, head),
            P(leaf, head),
            P(leaf, head),
            P(leaf, None),
            P(None, head),
            P(None, head),
            P(None, head),
            P(head, None),
            P(),
        ),
        out_specs=(
            P(leaf, head),
            P(leaf, head),
            P(leaf, head),
            P(leaf, head),
            P(head, leaf),
        ),
        check_vma=False,
    )
```

```python
import functools
import math

import jax
import jax.numpy as jnp
from jax import lax
from jax.experimental import pallas as pl
from jax.experimental.pallas import tpu as pltpu
from jax.sharding import Mesh, PartitionSpec as P

HEAD_WIDTH = 128
BLOCK = 128
GROUP = 2
NZ, NY = 8, 4
DEV_BLOCKS = 3
ROW_BLOCKS = NY * DEV_BLOCKS
COL_BLOCKS = NZ * DEV_BLOCKS
PATH = 16
PAIR = GROUP * BLOCK
SCALE = HEAD_WIDTH ** (-0.5)
SCALE2 = SCALE * math.log2(math.e)
NEG = -1e30
STAT_ROWS = 16
SLOTS = 2
UNROLL = 4
ENTRIES = 256
AT, SLOT, REACH, COUNT = 0, ENTRIES, 2 * ENTRIES, 3 * ENTRIES
PLAN = COUNT + 128

f32 = jnp.float32
bf16 = jnp.bfloat16


def dot_nt(a, b):
    return lax.dot_general(a, b, (((1,), (1,)), ((), ())), preferred_element_type=f32)


def dot_nn(a, b):
    return jnp.dot(a, b, preferred_element_type=f32)


def start_copies(pairs, sems, first=0):
    copies = [pltpu.make_async_copy(src, dst, sems.at[first + i]) for i, (src, dst) in enumerate(pairs)]
    for copy in copies:
        copy.start()
    return copies


def copy_all(pairs, sems):
    for copy in start_copies(pairs, sems):
        copy.wait()


def join_kernel(key_any, value_any, kv_ref, sems):
    copy_all(
        (
            (key_any, kv_ref.at[:, pl.ds(0, HEAD_WIDTH)]),
            (value_any, kv_ref.at[:, pl.ds(HEAD_WIDTH, HEAD_WIDTH)]),
        ),
        sems,
    )


def start_kernel(query_any, grad_any, weight_any, qd_ref, grad_ref, weight_ref, sems):
    pairs = ((grad_any, grad_ref), (weight_any, weight_ref), (query_any, qd_ref.at[:, pl.ds(0, PAIR)]))
    copies = start_copies(pairs, sems)
    copies[0].wait()
    copies[1].wait()
    qd_ref[:, PAIR:] = dot_nt(grad_ref[...], weight_ref[...]).astype(bf16)
    copies[2].wait()


def stack_kernel(own, before, after, top, bottom, out_ref, sems):
    y = lax.axis_index("y")
    pairs = []

    def put(src, src_row, back, row, count):
        at = lax.rem(y - back + NY, NY) * DEV_BLOCKS + row // BLOCK
        for k in range(2):
            for h in range(GROUP):
                src_cols = pl.ds(k * PAIR + h * HEAD_WIDTH, HEAD_WIDTH)
                dst = out_ref.at[at, pl.ds(h * BLOCK + row % BLOCK, count), pl.ds(k * HEAD_WIDTH, HEAD_WIDTH)]
                pairs.append((src.at[pl.ds(src_row, count), src_cols], dst))

    half = BLOCK // 2
    for src, back in ((own, 0), (before, 1), (after, 3)):
        for r in range(DEV_BLOCKS):
            put(src, r * BLOCK, back, r * BLOCK, BLOCK)
    put(top, 0, 2, 0, BLOCK)
    put(top, BLOCK, 2, BLOCK, half)
    put(bottom, 0, 2, BLOCK + half, half)
    put(bottom, half, 2, 2 * BLOCK, BLOCK)
    copy_all(pairs, sems)


def plan_kernel(anc_ref, plan_ref):
    z, y = lax.axis_index("z"), lax.axis_index("y")

    def put(e, at, slot, reach):
        plan_ref[AT + e] = at
        plan_ref[SLOT + e] = slot
        plan_ref[REACH + e] = reach

    def one_block(at, first):
        block = z * ROW_BLOCKS + at

        def one_key(j, e):
            c = anc_ref[j, block]
            device = lax.div(c, DEV_BLOCKS)
            row = lax.div(device, NY)
            hit = jnp.logical_and(c >= 0, device - row * NY == y)
            slot = row * DEV_BLOCKS + c - device * DEV_BLOCKS
            put(e, at, slot, jnp.where(c == block, 0, BLOCK))
            return e + hit.astype(jnp.int32)

        e = lax.fori_loop(0, PATH, one_key, first, unroll=True)
        put(e, at, 0, -BLOCK)
        return e + lax.rem(e, SLOTS)

    end = lax.fori_loop(0, ROW_BLOCKS, one_block, jnp.int32(0))
    for u in range(SLOTS * UNROLL):
        put(end + u, 0, 0, -BLOCK)
    plan_ref[COUNT] = lax.div(end, SLOTS)


def group_of(plan_ref, g):
    slots = [plan_ref[SLOT + SLOTS * g + k] for k in range(SLOTS)]
    reach = [plan_ref[REACH + SLOTS * g + k] for k in range(SLOTS)]
    return plan_ref[AT + SLOTS * g], slots, reach


def base2_scores(kv_ref, q, slots, reach):
    keys = jnp.concatenate([kv_ref[s, :, :HEAD_WIDTH] for s in slots], axis=0)
    s = dot_nt(keys, q) * SCALE2
    key_at = lax.broadcasted_iota(jnp.int32, (BLOCK, PAIR), 0)
    query_at = lax.rem(lax.broadcasted_iota(jnp.int32, (BLOCK, PAIR), 1), BLOCK)
    behind = key_at - query_at
    hide = jnp.concatenate([behind > r for r in reach], axis=0)
    return jnp.where(hide, NEG, s)


def value_dot(kv_ref, d, slots):
    return dot_nt(jnp.concatenate([kv_ref[s, :, HEAD_WIDTH:] for s in slots], axis=0), d)


def stats_kernel(plan_any, *refs):
    pieces, (qd_ref, out_ref, kv_ref, plan_ref, sems) = refs[:9], refs[9:]
    z = lax.axis_index("z")

    def slots_of(back):
        return pl.ds(lax.rem(z - back + NZ, NZ) * DEV_BLOCKS, DEV_BLOCKS)

    pairs = [(plan_any, plan_ref)]
    for piece, back in zip(pieces[:7], (0, 1, 2, 3, 5, 6, 7)):
        pairs.append((piece, kv_ref.at[slots_of(back)]))
    far = lax.rem(z + NZ // 2, NZ) * DEV_BLOCKS
    half = BLOCK // 2
    pairs.append((pieces[7].at[0:1], kv_ref.at[pl.ds(far, 1)]))
    pairs.append((pieces[7].at[1, pl.ds(0, half)], kv_ref.at[far + 1, pl.ds(0, half)]))
    pairs.append((pieces[8].at[0, pl.ds(half, half)], kv_ref.at[far + 1, pl.ds(half, half)]))
    pairs.append((pieces[8].at[1:2], kv_ref.at[pl.ds(far + 2, 1)]))
    copy_all(pairs, sems)
    out_ref[0:STAT_ROWS, :] = jnp.full((STAT_ROWS, PAIR), NEG, f32)
    out_ref[STAT_ROWS:, :] = jnp.zeros((2 * STAT_ROWS, PAIR), f32)

    def step(i, _):
        done = []
        for u in range(UNROLL):
            at, slots, reach = group_of(plan_ref, i * UNROLL + u)
            s = base2_scores(kv_ref, qd_ref[at, :, :HEAD_WIDTH], slots, reach)
            g = value_dot(kv_ref, qd_ref[at, :, HEAD_WIDTH:], slots)
            m = jnp.max(s, axis=0, keepdims=True)
            p = jnp.exp2(s - m)
            done.append((at, m, jnp.sum(p, axis=0, keepdims=True), jnp.sum(p * g, axis=0, keepdims=True)))
        for at, m, total, dsum in done:
            rows = [pl.ds(n * STAT_ROWS + at, 1) for n in range(3)]
            before = out_ref[rows[0], :]
            top = jnp.maximum(before, m)
            old, new = jnp.exp2(before - top), jnp.exp2(m - top)
            out_ref[rows[0], :] = top
            out_ref[rows[1], :] = out_ref[rows[1], :] * old + total * new
            out_ref[rows[2], :] = out_ref[rows[2], :] * old + dsum * new
        return 0

    lax.fori_loop(0, lax.div(plan_ref[COUNT] + UNROLL - 1, UNROLL), step, 0)


def grads_kernel(
    plan_any, kv_any, qd_any, st0, st1, st2, st3,
    row0, row1, row2, row3, col_any,
    o_scr, dq_scr, dk_scr, dv_scr, lse_scr, delta_scr,
    kv_ref, kvt_ref, qd_ref, plan_ref, row_scr, col_scr, sems,
):
    y = lax.axis_index("y")
    pairs = ((kv_any, kv_ref), (qd_any, qd_ref), (plan_any, plan_ref))
    copies = start_copies(pairs, sems)
    for scr in (o_scr, dq_scr, dk_scr, dv_scr):
        def clear(i, _, scr=scr):
            scr[i] = jnp.zeros(scr.shape[1:], f32)
            return 0

        lax.fori_loop(0, scr.shape[0], clear, 0)

    tops = [st[0:STAT_ROWS, :] for st in (st0, st1, st2, st3)]
    m = functools.reduce(jnp.maximum, tops)
    factors = [jnp.exp2(t - m) for t in tops]
    total, dsum = (
        sum(st[n * STAT_ROWS : (n + 1) * STAT_ROWS, :] * f for st, f in zip((st0, st1, st2, st3), factors))
        for n in (1, 2)
    )
    lse_scr[...] = m + jnp.log2(total)
    delta_scr[...] = dsum / total
    copies[0].wait()

    def turn(c, _):
        for k in range(2):
            cols = slice(k * HEAD_WIDTH, (k + 1) * HEAD_WIDTH)
            kvt_ref[c, cols, :] = kv_ref[c, :, cols].T
        return 0

    lax.fori_loop(0, COL_BLOCKS, turn, 0, unroll=4)
    for copy in copies[1:]:
        copy.wait()

    def step(i, _):
        done = []
        for u in range(UNROLL):
            at, slots, reach = group_of(plan_ref, i * UNROLL + u)
            q, d = qd_ref[at, :, :HEAD_WIDTH], qd_ref[at, :, HEAD_WIDTH:]
            w = jnp.exp2(base2_scores(kv_ref, q, slots, reach) - lse_scr[pl.ds(at, 1), :])
            g = value_dot(kv_ref, d, slots)
            p = w.astype(bf16)
            ds = (w * (g - delta_scr[pl.ds(at, 1), :]) * SCALE).astype(bf16)
            kt = jnp.concatenate([kvt_ref[s, :HEAD_WIDTH, :] for s in slots], axis=1)
            vt = jnp.concatenate([kvt_ref[s, HEAD_WIDTH:, :] for s in slots], axis=1)
            done.append((at, slots, dot_nn(vt, p), dot_nn(kt, ds), dot_nn(ds, q), dot_nn(p, d)))
        for at, slots, o, dq, dk, dv in done:
            o_scr[at] += o
            dq_scr[at] += dq
            for k, slot in enumerate(slots):
                dk_scr[slot] += dk[k * BLOCK : (k + 1) * BLOCK]
                dv_scr[slot] += dv[k * BLOCK : (k + 1) * BLOCK]
        return 0

    lax.fori_loop(0, lax.div(plan_ref[COUNT] + UNROLL - 1, UNROLL), step, 0)

    copies = []
    for n in range(NZ):
        for c in range(n * DEV_BLOCKS, (n + 1) * DEV_BLOCKS):
            col_scr[c, :, :HEAD_WIDTH] = dk_scr[c].astype(bf16)
            col_scr[c, :, HEAD_WIDTH:] = dv_scr[c].astype(bf16)
        part = pl.ds(n * DEV_BLOCKS, DEV_BLOCKS)
        copies += start_copies([(col_scr.at[part], col_any.at[part])], sems, 4 + n)
    for t, row_ref in enumerate((row0, row1, row2, row3)):
        for r in range(DEV_BLOCKS):
            at = lax.rem(y + t, NY) * DEV_BLOCKS + r
            cols = slice(r * BLOCK, (r + 1) * BLOCK)
            for h in range(GROUP):
                heads = slice(h * BLOCK, (h + 1) * BLOCK)
                rows = slice(h * HEAD_WIDTH, (h + 1) * HEAD_WIDTH)
                drows = slice(PAIR + h * HEAD_WIDTH, PAIR + (h + 1) * HEAD_WIDTH)
                row_scr[t, rows, cols] = o_scr[at, :, heads].astype(bf16)
                row_scr[t, drows, cols] = dq_scr[at, :, heads].astype(bf16)
        copies += start_copies([(row_scr.at[t], row_ref)], sems, 4 + NZ + t)
    for copy in copies:
        copy.wait()


def scatter_rows(part_ref, cols, value):
    y = lax.axis_index("y")
    step = value.shape[0] // (NZ * NY)
    value = value.astype(bf16)
    for i in range(NZ * NY):
        n, t = divmod(i, NY)
        part_ref[lax.rem(t - y + NY, NY), n * step : (n + 1) * step, cols] = value[i * step : (i + 1) * step]


def model_rows(i, nx, nc, width):
    head = lax.rem(lax.axis_index("x") + i % nx, nx) * nc + lax.rem(lax.axis_index("c") + i // nx, nc)
    return pl.ds(pl.multiple_of(head * width, width), width)


def rows_kernel(
    nx, nc, row0, row1, row2, row3, input_any, grad_any, wq_any, part_any, back_any, turned_any,
    got, input_ref, grad_ref, wq_ref, part_ref, back_ref, turned_ref, sems,
):
    pairs = [(row, got.at[t]) for t, row in enumerate((row0, row1, row2, row3))]
    pairs += [(input_any, input_ref), (grad_any, grad_ref), (wq_any, wq_ref)]
    copies = start_copies(pairs, sems)
    for copy in copies:
        copy.wait()
    turned_ref[...] = input_ref[...].T
    copies = start_copies([(turned_ref, turned_any)], sems, 7)
    o = sum(got[t, :PAIR, :].astype(f32) for t in range(NY)).astype(bf16)
    dq = sum(got[t, PAIR:, :].astype(f32) for t in range(NY)).astype(bf16)
    scatter_rows(part_ref, slice(0, PAIR), dot_nt(turned_ref[...], dq))
    scatter_rows(part_ref, slice(PAIR, 2 * PAIR), dot_nt(grad_ref[...].T, o))
    copies += start_copies([(part_ref, part_any)], sems, 8)
    width = wq_ref.shape[0] // (nx * nc)
    for i in range(nx * nc):
        back_ref[i * width : (i + 1) * width, :] = dot_nn(wq_ref[model_rows(i, nx, nc, width), :], dq)
    copies += start_copies([(back_ref, back_any)], sems, 9)
    for copy in copies:
        copy.wait()


def cols_kernel(got_any, turned_any, part_ref, d_ref, got_ref, turned_ref, sems):
    copies = start_copies(((got_any, got_ref), (turned_any, turned_ref)), sems)
    copies[0].wait()
    d_ref[...] = sum(got_ref[t].astype(f32) for t in range(NZ)).astype(bf16)
    copies[1].wait()
    scatter_rows(part_ref, slice(0, 2 * HEAD_WIDTH), dot_nn(turned_ref[...], d_ref[...]))


def back_kernel(nx, nc, d_ref, wk_any, wv_any, back_any, send_ref, keep_ref, wk_ref, wv_ref, back_ref, sems):
    copy_all(((wk_any, wk_ref), (wv_any, wv_ref), (back_any, back_ref)), sems)
    d = d_ref[...]
    width = wk_ref.shape[0] // (nx * nc)
    for i in range(nx * nc):
        rows = model_rows(i, nx, nc, width)
        w = jnp.concatenate([wk_ref[rows, :], wv_ref[rows, :]], axis=1)
        part = back_ref[i * width : (i + 1) * width, :] + dot_nt(w, d)
        if i < nx:
            keep_ref[i * width : (i + 1) * width, :] = part
        else:
            send_ref[(i - nx) * width : (i - nx + 1) * width, :] = part.astype(bf16)


SMEM_SPEC = pl.BlockSpec(memory_space=pltpu.SMEM)
VMEM_SPEC = pl.BlockSpec(memory_space=pltpu.VMEM)
HBM_SPEC = pl.BlockSpec(memory_space=pltpu.HBM)


def vmem(mib):
    return pltpu.CompilerParams(vmem_limit_bytes=mib * 1024 * 1024)


STACK = jax.ShapeDtypeStruct((ROW_BLOCKS, PAIR, 2 * HEAD_WIDTH), bf16)


def join_call(keys, values):
    return pl.pallas_call(
        join_kernel,
        out_shape=jax.ShapeDtypeStruct((keys.shape[0], 2 * HEAD_WIDTH), bf16),
        in_specs=[HBM_SPEC] * 2,
        out_specs=VMEM_SPEC,
        scratch_shapes=[pltpu.SemaphoreType.DMA((2,))],
        compiler_params=vmem(54),
        name="join",
    )(keys, values)


def start_call(queries, grad_out, output_weight):
    return pl.pallas_call(
        start_kernel,
        out_shape=jax.ShapeDtypeStruct((queries.shape[0], 2 * PAIR), bf16),
        in_specs=[HBM_SPEC] * 3,
        out_specs=VMEM_SPEC,
        scratch_shapes=[
            pltpu.VMEM(grad_out.shape, bf16),
            pltpu.VMEM(output_weight.shape, bf16),
            pltpu.SemaphoreType.DMA((3,)),
        ],
        compiler_params=vmem(54),
        name="start",
    )(queries, grad_out, output_weight)


def plan_call(anc):
    return pl.pallas_call(
        plan_kernel,
        out_shape=jax.ShapeDtypeStruct((PLAN,), jnp.int32),
        in_specs=[SMEM_SPEC],
        out_specs=SMEM_SPEC,
        name="plan",
    )(anc)


def stack_call(qds):
    return pl.pallas_call(
        stack_kernel,
        out_shape=STACK,
        in_specs=[HBM_SPEC] * 5,
        out_specs=HBM_SPEC,
        scratch_shapes=[pltpu.SemaphoreType.DMA((2 * GROUP * (3 * DEV_BLOCKS + 4),))],
        compiler_params=vmem(4),
        name="stack",
    )(*qds)


def stats_call(plan, pieces, qd):
    return pl.pallas_call(
        stats_kernel,
        out_shape=(
            jax.ShapeDtypeStruct((3 * STAT_ROWS, PAIR), f32),
            jax.ShapeDtypeStruct((COL_BLOCKS, BLOCK, 2 * HEAD_WIDTH), bf16),
        ),
        in_specs=[HBM_SPEC] * 10 + [VMEM_SPEC],
        out_specs=(VMEM_SPEC, VMEM_SPEC),
        scratch_shapes=[
            pltpu.SMEM((PLAN,), jnp.int32),
            pltpu.SemaphoreType.DMA((12,)),
        ],
        compiler_params=vmem(12),
        name="stats",
    )(plan, *pieces, qd)


def grads_call(plan, kv, qd, stats):
    return pl.pallas_call(
        grads_kernel,
        out_shape=(
            *[jax.ShapeDtypeStruct((2 * PAIR, DEV_BLOCKS * BLOCK), bf16)] * NY,
            jax.ShapeDtypeStruct((COL_BLOCKS, BLOCK, 2 * HEAD_WIDTH), bf16),
        ),
        in_specs=[HBM_SPEC] * 3 + [VMEM_SPEC] * 4,
        out_specs=(HBM_SPEC,) * 5,
        scratch_shapes=[
            pltpu.VMEM((ROW_BLOCKS, HEAD_WIDTH, PAIR), f32),
            pltpu.VMEM((ROW_BLOCKS, HEAD_WIDTH, PAIR), f32),
            pltpu.VMEM((COL_BLOCKS, BLOCK, HEAD_WIDTH), f32),
            pltpu.VMEM((COL_BLOCKS, BLOCK, HEAD_WIDTH), f32),
            pltpu.VMEM((STAT_ROWS, PAIR), f32),
            pltpu.VMEM((STAT_ROWS, PAIR), f32),
            pltpu.VMEM((COL_BLOCKS, BLOCK, 2 * HEAD_WIDTH), bf16),
            pltpu.VMEM((COL_BLOCKS, 2 * HEAD_WIDTH, BLOCK), bf16),
            pltpu.VMEM(STACK.shape, bf16),
            pltpu.SMEM((PLAN,), jnp.int32),
            pltpu.VMEM((NY, 2 * PAIR, DEV_BLOCKS * BLOCK), bf16),
            pltpu.VMEM((COL_BLOCKS, BLOCK, 2 * HEAD_WIDTH), bf16),
            pltpu.SemaphoreType.DMA((4 + NZ + NY,)),
        ],
        compiler_params=vmem(40),
        name="grads",
    )(plan, kv, qd, *stats)


def shift(x, axis, size, by):
    return lax.ppermute(x, axis, [(i, (i + by) % size) for i in range(size)])


def rows_call(nx, nc, got, normed_input, grad_out, query_weight):
    tokens, model = normed_input.shape
    return pl.pallas_call(
        functools.partial(rows_kernel, nx, nc),
        out_shape=(
            jax.ShapeDtypeStruct((NY, model // NY, 2 * PAIR), bf16),
            jax.ShapeDtypeStruct((model, tokens), f32),
            jax.ShapeDtypeStruct((model, tokens), bf16),
        ),
        in_specs=[HBM_SPEC] * 7,
        out_specs=(HBM_SPEC,) * 3,
        scratch_shapes=[
            pltpu.VMEM((NY, 2 * PAIR, tokens), bf16),
            pltpu.VMEM(normed_input.shape, bf16),
            pltpu.VMEM(normed_input.shape, bf16),
            pltpu.VMEM(query_weight.shape, bf16),
            pltpu.VMEM((NY, model // NY, 2 * PAIR), bf16),
            pltpu.VMEM((model, tokens), f32),
            pltpu.VMEM((model, tokens), bf16),
            pltpu.SemaphoreType.DMA((10,)),
        ],
        compiler_params=vmem(54),
        name="rows",
    )(*got, normed_input, grad_out, query_weight)


def cols_call(got, turned):
    model, tokens = turned.shape
    return pl.pallas_call(
        cols_kernel,
        out_shape=(
            jax.ShapeDtypeStruct((NY, model // NY, 2 * HEAD_WIDTH), bf16),
            jax.ShapeDtypeStruct((tokens, 2 * HEAD_WIDTH), bf16),
        ),
        in_specs=[HBM_SPEC] * 2,
        out_specs=(VMEM_SPEC,) * 2,
        scratch_shapes=[
            pltpu.VMEM(got.shape, bf16),
            pltpu.VMEM(turned.shape, bf16),
            pltpu.SemaphoreType.DMA((2,)),
        ],
        compiler_params=vmem(20),
        name="cols",
    )(got, turned)


def back_call(nx, nc, d, key_weight, value_weight, back):
    model, tokens = back.shape
    side = model // nc
    return pl.pallas_call(
        functools.partial(back_kernel, nx, nc),
        out_shape=(
            jax.ShapeDtypeStruct((max(model - side, side), tokens), bf16),
            jax.ShapeDtypeStruct((side, tokens), f32),
        ),
        in_specs=[VMEM_SPEC] + [HBM_SPEC] * 3,
        out_specs=(VMEM_SPEC,) * 2,
        scratch_shapes=[
            pltpu.VMEM(key_weight.shape, bf16),
            pltpu.VMEM(value_weight.shape, bf16),
            pltpu.VMEM(back.shape, f32),
            pltpu.SemaphoreType.DMA((3,)),
        ],
        compiler_params=vmem(20),
        name="back",
    )(d, key_weight, value_weight, back)


def finish_kernel(got_ref, q_ref, o_ref, k_ref, v_ref):
    total = sum(got_ref[t].astype(f32) for t in range(NZ))
    q_ref[...] = total[:, :PAIR]
    o_ref[...] = total[:, PAIR : 2 * PAIR]
    k_ref[...] = total[:, 2 * PAIR : 2 * PAIR + HEAD_WIDTH]
    v_ref[...] = total[:, 2 * PAIR + HEAD_WIDTH :]


def finish_call(got):
    rows = got.shape[1]
    return pl.pallas_call(
        finish_kernel,
        out_shape=tuple(jax.ShapeDtypeStruct((rows, n), f32) for n in (PAIR, PAIR, HEAD_WIDTH, HEAD_WIDTH)),
        in_specs=[VMEM_SPEC],
        out_specs=(VMEM_SPEC,) * 4,
        compiler_params=vmem(4),
        name="finish",
    )(got)


def ring_gather(own, plan):
    up, down = [own], [own]
    for step in range(3):
        up.append(shift(up[-1], "z", NZ, 1))
        down.append(shift(down[-1], "z", NZ, -1))
        if step == 1:
            up[-1], plan = lax.optimization_barrier((up[-1], plan))
    pieces = [p.reshape(DEV_BLOCKS, BLOCK, 2 * HEAD_WIDTH) for p in up + down[:0:-1]]
    top = shift(up[-1][: 2 * BLOCK], "z", NZ, 1)
    bottom = shift(down[-1][BLOCK:], "z", NZ, -1)
    return plan, pieces + [top.reshape(2, BLOCK, 2 * HEAD_WIDTH), bottom.reshape(2, BLOCK, 2 * HEAD_WIDTH)]


def per_device(
    nx, nc, normed_input, queries, keys, values, grad_out, query_weight, key_weight, value_weight, output_weight, ancestors
):
    model = grad_out.shape[1]

    plan, pieces = ring_gather(join_call(keys, values), plan_call(ancestors.T))
    mine = start_call(queries, grad_out, output_weight)
    before, after = shift(mine, "y", NY, 1), shift(mine, "y", NY, -1)
    half = mine.shape[0] // 2
    qds = [mine, before, after, shift(before[:half], "y", NY, 1), shift(after[half:], "y", NY, -1)]

    qd = stack_call(qds)
    own, kv = stats_call(plan, pieces, qd)
    stats = [own] + [shift(own, "y", NY, s) for s in range(1, NY)]
    *row_part, col_part = grads_call(plan, kv, qd, stats)

    col_got = lax.all_to_all(col_part.reshape(NZ, DEV_BLOCKS * BLOCK, 2 * HEAD_WIDTH), "z", 0, 0, tiled=True)
    row_got = [row_part[0]] + [shift(row_part[s], "y", NY, s) for s in range(1, NY)]

    part_rows = model // (NZ * NY)
    qo_part, back, turned = rows_call(nx, nc, row_got, normed_input, grad_out, query_weight)
    qo_got = [qo_part[0]] + [shift(qo_part[s], "y", NY, s) for s in range(1, NY)]

    kv_part, dkv = cols_call(col_got, turned)
    send, keep = back_call(nx, nc, dkv, key_weight, value_weight, back)
    kv_got = [kv_part[0]] + [shift(kv_part[s], "y", NY, s) for s in range(1, NY)]
    sums = [sum(g.astype(f32) for g in got).astype(bf16) for got in (qo_got, kv_got)]
    sums = jnp.concatenate(sums, axis=1).reshape(NZ, part_rows, 2 * PAIR + 2 * HEAD_WIDTH)
    q_grad, o_grad, k_grad, v_grad = finish_call(lax.all_to_all(sums, "z", 0, 0, tiled=True))

    width = model // (nx * nc)
    side = nx * width
    for s in range(1, nc):
        keep = keep + shift(send[(s - 1) * side : s * side], "c", nc, s).astype(f32)
    input_grad = keep[:width]
    for s in range(1, nx):
        piece = keep[s * width : (s + 1) * width].astype(bf16)
        input_grad = input_grad + shift(piece, "x", nx, s).astype(f32)
    return (
        input_grad.astype(bf16).T,
        q_grad,
        k_grad,
        v_grad,
        o_grad.T,
    )


def solution(mesh):
    heads = mesh.shape["head"]
    nc = 2 if heads % 2 == 0 else 1
    nx = heads // nc
    grid = Mesh(mesh.devices.reshape(NZ, NY, nx, nc), ("z", "y", "x", "c"))
    leaf, head = ("z", "y"), ("x", "c")
    return jax.shard_map(
        functools.partial(per_device, nx, nc),
        mesh=grid,
        in_specs=(
            P(leaf, None),
            P(leaf, head),
            P(leaf, head),
            P(leaf, head),
            P(leaf, None),
            P(None, head),
            P(None, head),
            P(None, head),
            P(head, None),
            P(),
        ),
        out_specs=(
            P(leaf, head),
            P(leaf, head),
            P(leaf, head),
            P(leaf, head),
            P(head, leaf),
        ),
        check_vma=False,
    )
```
